256 devices in a mesh: sect: 4 (over z_hi, core), ctx: 4 (over z_lo), tp: 16 (over y, x).
Axes of the slice: x: 4, y: 4, z: 8 (z_hi: 2, z_lo: 4; z = z_hi * 4 + z_lo), core: 2. Of those that a mesh axis runs over, the one named last changes fastest.
Arguments:
- span_queries: bfloat16 [4, 256, 8192], P('sect', 'ctx', 'tp'), may hold values from -15 to 15
- prompt_cache: bfloat16 [4, 2, 16384, 1024], P('sect', None, ('ctx', 'tp')), may hold values from -6 to 6
- span_kv: bfloat16 [4, 2, 256, 1024], P('sect', None, ('ctx', 'tp')), may hold values from -6 to 6
- span_offsets: int32 [4], P('sect'), may hold values from 0 to 16384, as said below
- decode_queries: bfloat16 [64, 8192], P(('sect', 'ctx'), 'tp'), may hold values from -12.5 to 12.5
- decode_cache: bfloat16 [64, 2, 2048, 1024], P(('sect', 'ctx'), None, 'tp'), may hold values from -6 to 6
- cache_lengths: int32 [64], P(('sect', 'ctx')), may hold values from 1 to 2048, as said below
- owner_rows: int32 [4], replicated, may hold values from 0 to 63, as said below
Outputs:
- span_attention: bfloat16 [4, 256, 8192], P('sect', 'ctx', 'tp')
- decode_attention: bfloat16 [64, 8192], P(('sect', 'ctx'), 'tp')
The draws below stay inside these ranges and needn't reach their ends.
Inputs may be any that keep to these rules, and one draw needn't show every extreme that they name: `span_offsets`: some request has exactly 16384. `cache_lengths`: some row has exactly 2048. `owner_rows`: all entries differ; some request goes to row 63.
All inputs are finite; a program needn't handle non-finite values.
Results may differ from the reference program's by a relative error of at most 0.0075.
Values may be sent and summed in bfloat16 or wider, within the bound.
A program may use at most 128 MiB of HBM per device.

```python
import math
import jax
import jax.numpy as jnp
from jax import lax

Q_HEADS = 64
KV_HEADS = 8
HEAD_DIM = 128
REQUESTS = 4
PROMPT = 16384
SPAN = 256
CACHE_LEN = 2048
ROWS = 64


def draw_span_queries(key, part):
    key = jax.random.fold_in(key, 11)
    base_key = jax.random.fold_in(key, 0)
    full_shape = (REQUESTS, SPAN, Q_HEADS * HEAD_DIM)
    values = jnp.clip(3.0 * jax.random.normal(base_key, full_shape, jnp.float32), -15.0, 15.0)
    return values.astype(jnp.bfloat16)


def draw_decode_queries(key, part):
    key = jax.random.fold_in(key, 12)
    base_key = jax.random.fold_in(key, 0)
    full_shape = (ROWS, Q_HEADS * HEAD_DIM)
    values = jnp.clip(2.5 * jax.random.normal(base_key, full_shape, jnp.float32), -12.5, 12.5)
    return values.astype(jnp.bfloat16)


def draw_prompt_cache(key, part):
    key = jax.random.fold_in(key, 13)
    base_key = jax.random.fold_in(key, 0)
    full_shape = (REQUESTS, 2, PROMPT, KV_HEADS * HEAD_DIM)
    values = jnp.clip(jax.random.normal(base_key, full_shape, jnp.float32), -6.0, 6.0)
    return values.astype(jnp.bfloat16)


def draw_span_kv(key, part):
    key = jax.random.fold_in(key, 14)
    base_key = jax.random.fold_in(key, 0)
    full_shape = (REQUESTS, 2, SPAN, KV_HEADS * HEAD_DIM)
    values = jnp.clip(jax.random.normal(base_key, full_shape, jnp.float32), -6.0, 6.0)
    return values.astype(jnp.bfloat16)


def draw_decode_cache(key, part):
    key = jax.random.fold_in(key, 15)
    base_key = jax.random.fold_in(key, 0)
    full_shape = (ROWS, 2, CACHE_LEN, KV_HEADS * HEAD_DIM)
    values = jnp.clip(jax.random.normal(base_key, full_shape, jnp.float32), -6.0, 6.0)
    return values.astype(jnp.bfloat16)


def draw_span_offsets(key, part):
    key = jax.random.fold_in(key, 21)
    base_key, spot_key = jax.random.split(key)
    drawn = jax.random.randint(base_key, (REQUESTS,), 0, PROMPT + 1)
    chosen_at = jax.random.randint(spot_key, (), 0, REQUESTS)
    return jnp.where(jnp.arange(REQUESTS) == chosen_at, PROMPT, drawn).astype(jnp.int32)


def draw_cache_lengths(key, part):
    key = jax.random.fold_in(key, 22)
    base_key, spot_key = jax.random.split(key)
    drawn = jax.random.randint(base_key, (ROWS,), 1, CACHE_LEN + 1)
    chosen_at = jax.random.randint(spot_key, (), 0, ROWS)
    return jnp.where(jnp.arange(ROWS) == chosen_at, CACHE_LEN, drawn).astype(jnp.int32)


def draw_owner_rows(key, part):
    key = jax.random.fold_in(key, 23)
    base_key, spot_key = jax.random.split(key)
    shuffled = jax.random.permutation(base_key, ROWS - 1)[:REQUESTS]
    chosen_at = jax.random.randint(spot_key, (), 0, REQUESTS)
    return jnp.where(jnp.arange(REQUESTS) == chosen_at, ROWS - 1, shuffled).astype(jnp.int32)


def setup_inputs(seed: int = 0) -> dict:
    key_of = jax.random.split(jax.random.key(seed), 9)
    return {
        "span_queries": draw_span_queries(jax.random.fold_in(key_of[8], 71), 0),
        "prompt_cache": draw_prompt_cache(jax.random.fold_in(key_of[8], 71), 0),
        "span_kv": draw_span_kv(jax.random.fold_in(key_of[8], 71), 0),
        "span_offsets": draw_span_offsets(jax.random.fold_in(key_of[8], 71), 0),
        "decode_queries": draw_decode_queries(jax.random.fold_in(key_of[8], 71), 0),
        "decode_cache": draw_decode_cache(jax.random.fold_in(key_of[8], 71), 0),
        "cache_lengths": draw_cache_lengths(jax.random.fold_in(key_of[8], 71), 0),
        "owner_rows": draw_owner_rows(jax.random.fold_in(key_of[8], 71), 0),
    }


masked_score = -1e+30

def attend_span(query_head, key_head, value_head, visible):
    score_scale = 1.0 / math.sqrt(HEAD_DIM)
    scores = jnp.einsum('tgd,pd->tgp', query_head, key_head) * score_scale
    scores = jnp.where(visible, scores, masked_score)
    row_max = lax.optimization_barrier(jnp.max(scores, axis=-1, keepdims=True))
    weights = jnp.where(visible, jnp.exp(scores - row_max), 0.0)
    row_sum = lax.optimization_barrier(jnp.sum(weights, axis=-1, keepdims=True))
    rounded = lax.optimization_barrier(weights.astype(jnp.bfloat16))
    weighted = jnp.einsum('tgp,pd->tgd', rounded.astype(jnp.float32), value_head)
    return weighted / row_sum

def attend_row(query_rows, key_rows, value_rows, visible):
    score_scale = 1.0 / math.sqrt(HEAD_DIM)
    scores = jnp.einsum('kgd,pkd->kgp', query_rows, key_rows) * score_scale
    allowed = visible[None, None, :]
    scores = jnp.where(allowed, scores, masked_score)
    row_max = lax.optimization_barrier(jnp.max(scores, axis=-1, keepdims=True))
    weights = jnp.where(allowed, jnp.exp(scores - row_max), 0.0)
    row_sum = lax.optimization_barrier(jnp.sum(weights, axis=-1, keepdims=True))
    rounded = lax.optimization_barrier(weights.astype(jnp.bfloat16))
    weighted = jnp.einsum('kgp,pkd->kgd', rounded.astype(jnp.float32), value_rows)
    return weighted / row_sum

def prefill_one(queries, cache, span_rows, offset):
    group_size = Q_HEADS // KV_HEADS
    span_len = queries.shape[0]
    prompt_len = cache.shape[1]
    grouped = queries.reshape(span_len, KV_HEADS, group_size, HEAD_DIM)
    keys_all = jnp.concatenate([cache[0], span_rows[0]], axis=0).reshape(prompt_len + span_len, KV_HEADS, HEAD_DIM)
    values_all = jnp.concatenate([cache[1], span_rows[1]], axis=0).reshape(prompt_len + span_len, KV_HEADS, HEAD_DIM)
    positions = jnp.arange(prompt_len + span_len, dtype=jnp.int32)
    tokens = jnp.arange(span_len, dtype=jnp.int32)
    visible = jnp.where(positions[None, :] < prompt_len, positions[None, :] < offset, positions[None, :] - prompt_len <= tokens[:, None])
    visible = visible[:, None, :]

    def one_head(head_index):
        query_head = lax.dynamic_index_in_dim(grouped, head_index, 1, keepdims=False).astype(jnp.float32)
        key_head = lax.dynamic_index_in_dim(keys_all, head_index, 1, keepdims=False).astype(jnp.float32)
        value_head = lax.dynamic_index_in_dim(values_all, head_index, 1, keepdims=False).astype(jnp.float32)
        return attend_span(query_head, key_head, value_head, visible)
    outputs = lax.map(one_head, jnp.arange(KV_HEADS, dtype=jnp.int32))
    return outputs.transpose(1, 0, 2, 3).reshape(span_len, Q_HEADS * HEAD_DIM).astype(jnp.bfloat16)

def decode_all(decode_queries, decode_cache, cache_lengths, span_kv, owner_rows):
    group_size = Q_HEADS // KV_HEADS
    row_total = decode_queries.shape[0]
    cache_len = decode_cache.shape[2]
    span_len = span_kv.shape[2]
    request_count = span_kv.shape[0]
    new_keys = span_kv[:, 0].reshape(request_count * span_len, KV_HEADS, HEAD_DIM).astype(jnp.float32)
    new_values = span_kv[:, 1].reshape(request_count * span_len, KV_HEADS, HEAD_DIM).astype(jnp.float32)
    key_owner = jnp.repeat(owner_rows, span_len)
    positions = jnp.arange(cache_len, dtype=jnp.int32)

    def one_row(row_index):
        query_rows = lax.dynamic_index_in_dim(decode_queries, row_index, 0, keepdims=False)
        query_rows = query_rows.reshape(KV_HEADS, group_size, HEAD_DIM).astype(jnp.float32)
        cache_rows = lax.dynamic_index_in_dim(decode_cache, row_index, 0, keepdims=False)
        key_rows = cache_rows[0].reshape(cache_len, KV_HEADS, HEAD_DIM).astype(jnp.float32)
        value_rows = cache_rows[1].reshape(cache_len, KV_HEADS, HEAD_DIM).astype(jnp.float32)
        length = lax.dynamic_index_in_dim(cache_lengths, row_index, 0, keepdims=False)
        keys_all = jnp.concatenate([key_rows, new_keys], axis=0)
        values_all = jnp.concatenate([value_rows, new_values], axis=0)
        visible = jnp.concatenate([positions < length, key_owner == row_index])
        return attend_row(query_rows, keys_all, values_all, visible)
    outputs = lax.map(one_row, jnp.arange(row_total, dtype=jnp.int32))
    return outputs.reshape(row_total, Q_HEADS * HEAD_DIM).astype(jnp.bfloat16)

def reference(span_queries, prompt_cache, span_kv, span_offsets, decode_queries, decode_cache, cache_lengths, owner_rows):
    span_attention = jnp.stack([prefill_one(span_queries[request], prompt_cache[request], span_kv[request], span_offsets[request]) for request in range(REQUESTS)])
    decode_attention = decode_all(decode_queries, decode_cache, cache_lengths, span_kv, owner_rows)
    return (span_attention, decode_attention)
```

```python
import math

import jax
import jax.numpy as jnp
from jax import lax
from jax.experimental import pallas as pl
from jax.experimental.pallas import tpu as pltpu
from jax.sharding import PartitionSpec as P

HEAD_DIM = 128
MESH = pl.DeviceIdType.MESH
NEG = -1e30
EXP2_SCALE = math.log2(math.e) / math.sqrt(HEAD_DIM)
F32 = jnp.float32
BF16 = jnp.bfloat16


def dot_nt(a, b):
    return lax.dot_general(a, b, (((1,), (1,)), ((), ())), preferred_element_type=F32)


def dot_nn(a, b):
    return lax.dot_general(a, b, (((1,), (0,)), ((), ())), preferred_element_type=F32)


def iota(shape, dim):
    return lax.broadcasted_iota(jnp.int32, shape, dim)


def select4(index, values):
    return jnp.where(
        index == 0,
        values[0],
        jnp.where(index == 1, values[1], jnp.where(index == 2, values[2], values[3])),
    )


def kernel(
    off_ref,
    len_ref,
    own_ref,
    dq_ref,
    skv_ref,
    q_hbm,
    pc_hbm,
    dc_hbm,
    out_ref,
    dout_ref,
    cache,
    kv,
    vt,
    q_all,
    scores,
    po_send,
    po_recv,
    ps_send,
    ps_recv,
    sp_head,
    sp_pre,
    sp_block,
    sp_all,
    sp_wide,
    dq_wide,
    dq_block,
    dq_all,
    dp_send,
    dp_recv,
    d_result,
    local_sem,
    kv_ssem,
    kv_rsem,
    q_ssem,
    q_rsem,
    sp_ssem,
    sp_rsem,
    sa_ssem,
    sa_rsem,
    dq_ssem,
    dq_rsem,
    dp_ssem,
    dp_rsem,
    po_ssem,
    po_rsem,
    ps_ssem,
    ps_rsem,
):
    s = lax.axis_index("sect")
    c = lax.axis_index("ctx")
    t = lax.axis_index("tp")
    y = t // 4
    x = t % 4
    head = t // 2
    pair = t + 1 - 2 * (t % 2)

    def kv_peer(slot, sign):
        a, b = slot // 2, slot % 2
        far_y = (y + sign * a + 4) % 4
        far_x = x + b * (3 - 2 * x)
        return far_y * 4 + far_x

    def q_peer(slot, sign):
        a, b = slot // 2, slot % 2
        return (c + sign * a + 4) % 4, t + b * (pair - t)

    def span_peer(step):
        g = (s * 4 + c + step) % 16
        return g // 4, g % 4

    def kv_copy(slot):
        far = kv_peer(slot, 1)
        column = pl.multiple_of((far // 2) * HEAD_DIM, HEAD_DIM)
        return pltpu.make_async_remote_copy(
            src_ref=pc_hbm.at[0, :, :, pl.ds(column, HEAD_DIM)],
            dst_ref=kv.at[slot],
            send_sem=kv_ssem.at[slot],
            recv_sem=kv_rsem.at[slot],
            device_id=(s, c, far),
            device_id_type=MESH,
        )

    def q_copy(slot):
        far_c, far_t = q_peer(slot, 1)
        return pltpu.make_async_remote_copy(
            src_ref=q_hbm.at[0],
            dst_ref=q_all.at[slot],
            send_sem=q_ssem.at[slot],
            recv_sem=q_rsem.at[slot],
            device_id=(s, far_c, far_t),
            device_id_type=MESH,
        )

    def sp_copy(slot):
        far = kv_peer(slot, 1)
        return pltpu.make_async_remote_copy(
            src_ref=sp_head.at[far // 2],
            dst_ref=sp_pre.at[slot],
            send_sem=sp_ssem.at[slot],
            recv_sem=sp_rsem.at[slot],
            device_id=(s, c, far),
            device_id_type=MESH,
        )

    def sa_copy(step):
        far_s, far_c = span_peer(step)
        return pltpu.make_async_remote_copy(
            src_ref=sp_block,
            dst_ref=sp_all.at[s * 4 + c],
            send_sem=sa_ssem.at[step],
            recv_sem=sa_rsem.at[step],
            device_id=(far_s, far_c, t),
            device_id_type=MESH,
        )

    def dq_copy(step):
        return pltpu.make_async_remote_copy(
            src_ref=dq_block,
            dst_ref=dq_all.at[t],
            send_sem=dq_ssem.at[step],
            recv_sem=dq_rsem.at[step],
            device_id=(s, c, (t + step) % 16),
            device_id_type=MESH,
        )

    def dp_copy(step):
        far = (t + step) % 16
        return pltpu.make_async_remote_copy(
            src_ref=dp_send.at[far],
            dst_ref=dp_recv.at[step],
            send_sem=dp_ssem.at[step],
            recv_sem=dp_rsem.at[step],
            device_id=(s, c, far),
            device_id_type=MESH,
        )

    def po_copy(slot):
        far_c, far_t = q_peer(slot, -1)
        return pltpu.make_async_remote_copy(
            src_ref=po_send.at[slot],
            dst_ref=po_recv.at[slot],
            send_sem=po_ssem.at[slot],
            recv_sem=po_rsem.at[slot],
            device_id=(s, far_c, far_t),
            device_id_type=MESH,
        )

    def ps_copy(slot):
        far_c, far_t = q_peer(slot, -1)
        return pltpu.make_async_remote_copy(
            src_ref=ps_send.at[slot],
            dst_ref=ps_recv.at[slot],
            send_sem=ps_ssem.at[slot],
            recv_sem=ps_rsem.at[slot],
            device_id=(s, far_c, far_t),
            device_id_type=MESH,
        )

    own_column = pl.multiple_of(head * HEAD_DIM, HEAD_DIM)
    local_kv = pltpu.make_async_copy(
        pc_hbm.at[0, :, :, pl.ds(own_column, HEAD_DIM)], kv.at[0], local_sem.at[0]
    )
    local_q = pltpu.make_async_copy(q_hbm.at[0], q_all.at[0], local_sem.at[1])
    local_cache = pltpu.make_async_copy(dc_hbm, cache, local_sem.at[2])
    local_kv.start()
    local_q.start()
    local_cache.start()

    barrier = pltpu.get_barrier_semaphore()

    def greet(far_s, far_c, far_t):
        pl.semaphore_signal(
            barrier, inc=1, device_id=(far_s, far_c, far_t), device_id_type=MESH
        )

    for step in range(1, 16):
        greet(s, c, (t + step) % 16)
        far_s, far_c = span_peer(step)
        greet(far_s, far_c, t)
    for step in range(1, 4):
        greet(s, (c + step) % 4, pair)

    own_q = dq_ref[...].astype(F32)
    span_k = skv_ref[0, 0].astype(F32)
    span_v = skv_ref[0, 1].astype(F32)
    for h in range(4):
        dq_wide[4 * h : 4 * h + 4, :] = own_q[:, h * HEAD_DIM : (h + 1) * HEAD_DIM]
    for h in range(8):
        sp_head[h, 0:4, :] = span_k[:, h * HEAD_DIM : (h + 1) * HEAD_DIM]
        sp_head[h, 4:8, :] = span_v[:, h * HEAD_DIM : (h + 1) * HEAD_DIM]
    dq_block[...] = dq_wide[...].astype(BF16)
    sp_block[...] = sp_head[...].reshape(64, HEAD_DIM).astype(BF16)

    pl.semaphore_wait(barrier, 33)

    for step in range(1, 16):
        dq_copy(step).start()
    for slot in range(1, 8):
        kv_copy(slot).start()
        q_copy(slot).start()
        sp_copy(slot).start()
    for step in range(1, 16):
        sa_copy(step).start()

    dq_all[t] = dq_block[...]
    sp_all[s * 4 + c] = sp_block[...]
    sp_pre[0] = sp_head[head]

    local_cache.wait()
    for step in range(1, 16):
        dq_copy(step).wait_recv()
    for step in range(1, 16):
        sa_copy(step).wait_recv()
    sp_wide[...] = sp_all[...].astype(F32)
    row_q = iota((32, 512), 0) % 4
    row_p = iota((32, 512), 1) // 128
    pos = t * 128 + iota((32, 512), 1) % 128
    length = select4(row_p, [len_ref[r] for r in range(4)])
    cache_live = (row_q == row_p) & (pos < length)
    new_col = iota((32, 128), 1)
    new_owner = select4(new_col // 32, [own_ref[r] for r in range(4)])
    new_row = (s * 4 + c) * 4 + iota((32, 128), 0) % 4
    new_live = (new_owner == new_row) & (new_col % 8 < 4)

    def decode_head(k, carry):
        column = pl.ds(pl.multiple_of(k * HEAD_DIM, HEAD_DIM), HEAD_DIM)
        queries = dq_all[pl.ds(2 * k, 2)].reshape(32, HEAD_DIM)
        fresh = (
            sp_wide[:, pl.ds(pl.multiple_of(8 * k, 8), 8), :].reshape(128, HEAD_DIM).astype(BF16)
        )
        part = jnp.concatenate(
            [dot_nt(queries, cache[r, 0, :, column]) for r in range(4)], axis=1
        )
        part = jnp.where(cache_live, part, NEG)
        fresh_part = jnp.where(new_live, dot_nt(queries, fresh), NEG)
        top = jnp.maximum(
            jnp.max(part, axis=1, keepdims=True), jnp.max(fresh_part, axis=1, keepdims=True)
        )
        part = jnp.exp2((part - top) * EXP2_SCALE)
        fresh_part = jnp.exp2((fresh_part - top) * EXP2_SCALE)
        fresh_part = jnp.where(new_live, fresh_part, 0.0)
        total = jnp.sum(part, axis=1, keepdims=True) + jnp.sum(fresh_part, axis=1, keepdims=True)
        rounded = part.astype(BF16)
        acc = dot_nn(pltpu.roll(fresh_part, 4, axis=1).astype(BF16), fresh)
        for r in range(4):
            acc += dot_nn(rounded[:, r * 128 : (r + 1) * 128], cache[r, 1, :, column])
        stats = jnp.where(iota((32, 128), 1) < 64, top, total)
        dp_send[pl.ds(2 * k, 2), 0] = acc.reshape(2, 16, HEAD_DIM)
        dp_send[pl.ds(2 * k, 2), 1] = stats.reshape(2, 16, HEAD_DIM)
        return carry

    lax.fori_loop(0, 8, decode_head, 0)
    for step in range(1, 16):
        dp_copy(step).start()

    local_kv.wait()
    local_q.wait()
    for slot in range(1, 8):
        sp_copy(slot).wait_recv()
    for slot in range(1, 8):
        kv_copy(slot).wait_recv()
    for slot in range(8):
        vt[:, slot * 256 : (slot + 1) * 256] = kv[slot, 1].astype(F32).T.astype(BF16)
    span_rows = sp_pre[...].reshape(64, HEAD_DIM)
    span_keys = span_rows.astype(BF16)
    span_vt = pltpu.roll(span_rows, 60, axis=0).T.astype(BF16)
    offset = off_ref[0]
    span_row = iota((64, 256), 0)
    span_slot = span_row // 8
    span_y = (y - span_slot // 2 + 4) % 4
    span_x = x + (span_slot % 2) * (3 - 2 * x)
    span_token = (c * 16 + span_y * 4 + span_x) * 4 + span_row % 8
    span_real = span_row % 8 < 4

    def chunk(i, carry):
        slot = 7 - i
        far_c, _ = q_peer(slot, -1)

        @pl.when(slot > 0)
        def _():
            q_copy(slot).wait_recv()

        block = q_all[slot]
        queries = jnp.concatenate(
            [block[:, h * HEAD_DIM : (h + 1) * HEAD_DIM] for h in range(4)], axis=0
        )
        span_live = span_real & (span_token <= far_c * 64 + iota((64, 256), 1) % 64)
        span_part = jnp.where(span_live, dot_nt(span_keys, queries), NEG)
        top = jnp.max(span_part.reshape(8, 8, 256), axis=0)
        for b in range(8):
            start = (c * 16 + kv_peer(b, -1)) * 256
            part = dot_nt(kv[b, 0], queries)
            part = jnp.where(start + iota((256, 256), 0) < offset, part, NEG)
            scores[b] = part
            top = jnp.maximum(top, jnp.max(part.reshape(32, 8, 256), axis=0))
        top = jnp.max(top, axis=0, keepdims=True)
        weights = jnp.where(span_live, jnp.exp2((span_part - top) * EXP2_SCALE), 0.0)
        total = jnp.sum(weights.reshape(8, 8, 256), axis=0)
        acc = dot_nn(span_vt, weights.astype(BF16))
        for b in range(8):
            weights = jnp.exp2((scores[b] - top) * EXP2_SCALE)
            total += jnp.sum(weights.reshape(32, 8, 256), axis=0)
            acc += dot_nn(vt[:, b * 256 : (b + 1) * 256], weights.astype(BF16))
        total = jnp.sum(total, axis=0, keepdims=True)
        po_send[slot] = acc.astype(BF16)
        ps_send[slot] = jnp.where(iota((8, 256), 0) < 4, top, total)

        @pl.when(slot > 0)
        def _():
            po_copy(slot).start()
            ps_copy(slot).start()

        return carry

    lax.fori_loop(0, 8, chunk, 0)

    for step in range(1, 16):
        dp_copy(step).wait_recv()
    dp_recv[0] = dp_send[t]
    tops = [dp_recv[i, 1][:, 0:1] for i in range(16)]
    top = tops[0]
    for i in range(1, 16):
        top = jnp.maximum(top, tops[i])
    acc = jnp.zeros((16, HEAD_DIM), F32)
    total = jnp.zeros((16, 1), F32)
    for i in range(16):
        factor = jnp.exp2((tops[i] - top) * EXP2_SCALE)
        acc += dp_recv[i, 0] * factor
        total += dp_recv[i, 1][:, 64:65] * factor
    d_result[...] = acc / total
    for h in range(4):
        dout_ref[:, h * HEAD_DIM : (h + 1) * HEAD_DIM] = d_result[4 * h : 4 * h + 4, :].astype(BF16)

    for slot in range(1, 8):
        ps_copy(slot).wait_recv()
        po_copy(slot).wait_recv()
    ps_recv[0] = ps_send[0]
    po_recv[0] = po_send[0]
    top = ps_recv[0, 0:1, :]
    for i in range(1, 8):
        top = jnp.maximum(top, ps_recv[i, 0:1, :])
    acc = jnp.zeros((HEAD_DIM, 256), F32)
    total = jnp.zeros((1, 256), F32)
    for i in range(8):
        factor = jnp.exp2((ps_recv[i, 0:1, :] - top) * EXP2_SCALE)
        acc += po_recv[i].astype(F32) * factor
        total += ps_recv[i, 4:5, :] * factor
    result = (acc / total).T
    for h in range(4):
        out_ref[0, :, h * HEAD_DIM : (h + 1) * HEAD_DIM] = result[h * 64 : (h + 1) * 64].astype(BF16)

    for step in range(1, 16):
        dq_copy(step).wait_send()
        sa_copy(step).wait_send()
        dp_copy(step).wait_send()
    for slot in range(1, 8):
        kv_copy(slot).wait_send()
        q_copy(slot).wait_send()
        sp_copy(slot).wait_send()
        po_copy(slot).wait_send()
        ps_copy(slot).wait_send()


def body(
    span_queries,
    prompt_cache,
    span_kv,
    span_offsets,
    decode_queries,
    decode_cache,
    cache_lengths,
    owner_rows,
):
    smem = pl.BlockSpec(memory_space=pltpu.SMEM)
    vmem = pl.BlockSpec(memory_space=pltpu.VMEM)
    hbm = pl.BlockSpec(memory_space=pl.ANY)
    sem = pltpu.SemaphoreType.DMA
    return pl.pallas_call(
        kernel,
        out_shape=(
            jax.ShapeDtypeStruct(span_queries.shape, BF16),
            jax.ShapeDtypeStruct(decode_queries.shape, BF16),
        ),
        in_specs=[smem, smem, smem, vmem, vmem, hbm, hbm, hbm],
        out_specs=(vmem, vmem),
        scratch_shapes=[
            pltpu.VMEM((4, 2, 128, 1024), BF16),
            pltpu.VMEM((8, 2, 256, HEAD_DIM), BF16),
            pltpu.VMEM((HEAD_DIM, 2048), BF16),
            pltpu.VMEM((8, 64, 512), BF16),
            pltpu.VMEM((8, 256, 256), F32),
            pltpu.VMEM((8, HEAD_DIM, 256), BF16),
            pltpu.VMEM((8, HEAD_DIM, 256), BF16),
            pltpu.VMEM((8, 8, 256), F32),
            pltpu.VMEM((8, 8, 256), F32),
            pltpu.VMEM((8, 8, HEAD_DIM), F32),
            pltpu.VMEM((8, 8, HEAD_DIM), F32),
            pltpu.VMEM((64, HEAD_DIM), BF16),
            pltpu.VMEM((16, 64, HEAD_DIM), BF16),
            pltpu.VMEM((16, 64, HEAD_DIM), F32),
            pltpu.VMEM((16, HEAD_DIM), F32),
            pltpu.VMEM((16, HEAD_DIM), BF16),
            pltpu.VMEM((16, 16, HEAD_DIM), BF16),
            pltpu.VMEM((16, 2, 16, HEAD_DIM), F32),
            pltpu.VMEM((16, 2, 16, HEAD_DIM), F32),
            pltpu.VMEM((16, HEAD_DIM), F32),
            sem((3,)),
            sem((8,)),
            sem((8,)),
            sem((8,)),
            sem((8,)),
            sem((8,)),
            sem((8,)),
            sem((16,)),
            sem((16,)),
            sem((16,)),
            sem((16,)),
            sem((16,)),
            sem((16,)),
            sem((8,)),
            sem((8,)),
            sem((8,)),
            sem((8,)),
        ],
        compiler_params=pltpu.CompilerParams(
            collective_id=0, has_side_effects=True, vmem_limit_bytes=48 * 1024 * 1024
        ),
    )(
        span_offsets,
        cache_lengths,
        owner_rows,
        decode_queries,
        span_kv,
        span_queries,
        prompt_cache,
        decode_cache,
    )


def solution(mesh):
    return jax.shard_map(
        body,
        mesh=mesh,
        in_specs=(
            P("sect", "ctx", "tp"),
            P("sect", None, ("ctx", "tp"), None),
            P("sect", None, ("ctx", "tp"), None),
            P("sect"),
            P(("sect", "ctx"), "tp"),
            P(("sect", "ctx"), None, "tp", None),
            P(("sect", "ctx")),
            P(),
        ),
        out_specs=(P("sect", "ctx", "tp"), P(("sect", "ctx"), "tp")),
        check_vma=False,
    )
```

```python
import math

import jax
import jax.numpy as jnp
from jax import lax
from jax.experimental import pallas as pl
from jax.experimental.pallas import tpu as pltpu
from jax.sharding import PartitionSpec as P

HEAD_DIM = 128
MESH = pl.DeviceIdType.MESH
NEG = -1e30
EXP2_SCALE = math.log2(math.e) / math.sqrt(HEAD_DIM)
F32 = jnp.float32
BF16 = jnp.bfloat16
NEAR = (0, 1, 2, 6, 3, 7)
FAR = (4, 5)


def dot_nt(a, b):
    return lax.dot_general(a, b, (((1,), (1,)), ((), ())), preferred_element_type=F32)


def dot_nn(a, b):
    return lax.dot_general(a, b, (((1,), (0,)), ((), ())), preferred_element_type=F32)


def iota(shape, dim):
    return lax.broadcasted_iota(jnp.int32, shape, dim)


def select4(index, values):
    return jnp.where(
        index == 0,
        values[0],
        jnp.where(index == 1, values[1], jnp.where(index == 2, values[2], values[3])),
    )


def kernel(
    off_hbm,
    len_hbm,
    own_hbm,
    dq_hbm,
    skv_hbm,
    q_hbm,
    pc_hbm,
    dc_hbm,
    out_ref,
    dout_ref,
    off_ref,
    len_ref,
    own_ref,
    dq_ref,
    skv_ref,
    cache,
    kv,
    vt,
    q_all,
    scores,
    run_top,
    run_total,
    run_acc,
    po_send,
    po_recv,
    ps_send,
    ps_recv,
    sp_head,
    sp_pre,
    sp_block,
    sp_all,
    sp_wide,
    dq_wide,
    dq_block,
    dq_all,
    dp_send,
    dp_recv,
    d_result,
    local_sem,
    kv_ssem,
    kv_rsem,
    q_ssem,
    q_rsem,
    sp_ssem,
    sp_rsem,
    sa_ssem,
    sa_rsem,
    dq_ssem,
    dq_rsem,
    dp_ssem,
    dp_rsem,
    po_ssem,
    po_rsem,
    ps_ssem,
    ps_rsem,
):
    s = lax.axis_index("sect")
    c = lax.axis_index("ctx")
    t = lax.axis_index("tp")
    y = t // 4
    x = t % 4
    head = t // 2
    pair = t + 1 - 2 * (t % 2)

    def kv_peer(slot, sign):
        a, b = slot // 2, slot % 2
        far_y = (y + sign * a + 4) % 4
        far_x = x + b * (3 - 2 * x)
        return far_y * 4 + far_x

    def q_peer(slot, sign):
        a, b = slot // 2, slot % 2
        return (c + sign * a + 4) % 4, t + b * (pair - t)

    core = s % 2
    layer = (s // 2) * 4 + c

    def span_peer(step):
        far = (layer + step) % 8
        return (far // 4) * 2 + core, far % 4

    def kv_copy(slot):
        far = kv_peer(slot, 1)
        column = pl.multiple_of((far // 2) * HEAD_DIM, HEAD_DIM)
        return pltpu.make_async_remote_copy(
            src_ref=pc_hbm.at[0, :, :, pl.ds(column, HEAD_DIM)],
            dst_ref=kv.at[slot],
            send_sem=kv_ssem.at[slot],
            recv_sem=kv_rsem.at[slot],
            device_id=(s, c, far),
            device_id_type=MESH,
        )

    def q_copy(step):
        return pltpu.make_async_remote_copy(
            src_ref=q_hbm.at[0],
            dst_ref=q_all.at[2 * step],
            send_sem=q_ssem.at[2 * step],
            recv_sem=q_rsem.at[2 * step],
            device_id=(s, (c + step) % 4, t),
            device_id_type=MESH,
        )

    def q_forward(step):
        return pltpu.make_async_remote_copy(
            src_ref=q_all.at[2 * step],
            dst_ref=q_all.at[2 * step + 1],
            send_sem=q_ssem.at[2 * step + 1],
            recv_sem=q_rsem.at[2 * step + 1],
            device_id=(s, c, pair),
            device_id_type=MESH,
        )

    def sp_copy(slot):
        far = kv_peer(slot, 1)
        return pltpu.make_async_remote_copy(
            src_ref=sp_head.at[far // 2],
            dst_ref=sp_pre.at[slot],
            send_sem=sp_ssem.at[slot],
            recv_sem=sp_rsem.at[slot],
            device_id=(s, c, far),
            device_id_type=MESH,
        )

    def sa_copy(step):
        far_s, far_c = span_peer(step)
        return pltpu.make_async_remote_copy(
            src_ref=sp_block,
            dst_ref=sp_all.at[s // 2, core, c],
            send_sem=sa_ssem.at[step],
            recv_sem=sa_rsem.at[step],
            device_id=(far_s, far_c, t),
            device_id_type=MESH,
        )

    def sa_forward():
        return pltpu.make_async_remote_copy(
            src_ref=sp_all.at[:, core],
            dst_ref=sp_all.at[:, core],
            send_sem=sa_ssem.at[0],
            recv_sem=sa_rsem.at[0],
            device_id=(s + 1 - 2 * core, c, t),
            device_id_type=MESH,
        )

    def dq_copy(step):
        return pltpu.make_async_remote_copy(
            src_ref=dq_block,
            dst_ref=dq_all.at[t],
            send_sem=dq_ssem.at[step],
            recv_sem=dq_rsem.at[step],
            device_id=(s, c, (t + step) % 16),
            device_id_type=MESH,
        )

    def dp_copy(step):
        far = (t + step) % 16
        return pltpu.make_async_remote_copy(
            src_ref=dp_send.at[far],
            dst_ref=dp_recv.at[step],
            send_sem=dp_ssem.at[step],
            recv_sem=dp_rsem.at[step],
            device_id=(s, c, far),
            device_id_type=MESH,
        )

    def po_copy(slot):
        far_c, far_t = q_peer(slot, -1)
        return pltpu.make_async_remote_copy(
            src_ref=po_send.at[slot],
            dst_ref=po_recv.at[slot],
            send_sem=po_ssem.at[slot],
            recv_sem=po_rsem.at[slot],
            device_id=(s, far_c, far_t),
            device_id_type=MESH,
        )

    def ps_copy(slot):
        far_c, far_t = q_peer(slot, -1)
        return pltpu.make_async_remote_copy(
            src_ref=ps_send.at[slot],
            dst_ref=ps_recv.at[slot],
            send_sem=ps_ssem.at[slot],
            recv_sem=ps_rsem.at[slot],
            device_id=(s, far_c, far_t),
            device_id_type=MESH,
        )

    barrier = pltpu.get_barrier_semaphore()

    def greet(far_s, far_c, far_t):
        pl.semaphore_signal(
            barrier, inc=1, device_id=(far_s, far_c, far_t), device_id_type=MESH
        )

    for step in range(1, 8):
        far_s, far_c = span_peer(step)
        greet(far_s, far_c, t)
    for step in range(1, 16):
        greet(s, c, (t + step) % 16)
    for step in range(1, 4):
        greet(s, (c + step) % 4, pair)
    greet(s + 1 - 2 * core, c, t)

    own_column = pl.multiple_of(head * HEAD_DIM, HEAD_DIM)
    local_small = [
        pltpu.make_async_copy(source, target, local_sem.at[3 + i])
        for i, (source, target) in enumerate(
            [
                (dq_hbm, dq_ref),
                (skv_hbm, skv_ref),
                (off_hbm, off_ref),
                (len_hbm, len_ref),
                (own_hbm, own_ref),
            ]
        )
    ]
    for copy in local_small:
        copy.start()
    local_kv = pltpu.make_async_copy(
        pc_hbm.at[0, :, :, pl.ds(own_column, HEAD_DIM)], kv.at[0], local_sem.at[0]
    )
    local_q = pltpu.make_async_copy(q_hbm.at[0], q_all.at[0], local_sem.at[1])
    local_cache = pltpu.make_async_copy(dc_hbm, cache, local_sem.at[2])
    local_q.start()
    local_kv.start()
    local_cache.start()

    for copy in local_small:
        copy.wait()
    own_q = dq_ref[...].astype(F32)
    span_k = skv_ref[0, 0].astype(F32)
    span_v = skv_ref[0, 1].astype(F32)
    for h in range(4):
        dq_wide[4 * h : 4 * h + 4, :] = own_q[:, h * HEAD_DIM : (h + 1) * HEAD_DIM]
    for h in range(8):
        sp_head[h, 0:4, :] = span_k[:, h * HEAD_DIM : (h + 1) * HEAD_DIM]
        sp_head[h, 4:8, :] = span_v[:, h * HEAD_DIM : (h + 1) * HEAD_DIM]
    dq_block[...] = dq_wide[...].astype(BF16)
    sp_block[...] = sp_head[...].reshape(64, HEAD_DIM).astype(BF16)
    dq_all[t] = dq_block[...]
    sp_all[s // 2, core, c] = sp_block[...]
    sp_pre[0] = sp_head[head]
    local_q.wait()

    pl.semaphore_wait(barrier, 26)

    for step in range(1, 16):
        dq_copy(step).start()
    for slot in NEAR[1:]:
        kv_copy(slot).start()
    q_forward(0).start()
    for step in range(1, 4):
        q_copy(step).start()
    for slot in FAR:
        kv_copy(slot).start()
    for slot in range(1, 8):
        sp_copy(slot).start()

    local_cache.wait()
    for step in range(1, 16):
        dq_copy(step).wait_recv()
    row_q = iota((32, 512), 0) % 4
    row_p = iota((32, 512), 1) // 128
    pos = t * 128 + iota((32, 512), 1) % 128
    length = select4(row_p, [len_ref[r] for r in range(4)])
    cache_live = (row_q == row_p) & (pos < length)
    left = iota((32, 128), 1) < 64

    def decode_cached(k, carry):
        column = pl.ds(pl.multiple_of(k * HEAD_DIM, HEAD_DIM), HEAD_DIM)
        queries = dq_all[pl.ds(2 * k, 2)].reshape(32, HEAD_DIM)
        part = jnp.concatenate(
            [dot_nt(queries, cache[r, 0, :, column]) for r in range(4)], axis=1
        )
        part = jnp.where(cache_live, part, NEG)
        top = jnp.max(part, axis=1, keepdims=True)
        part = jnp.exp2((part - top) * EXP2_SCALE)
        total = jnp.sum(part, axis=1, keepdims=True)
        rounded = part.astype(BF16)
        acc = jnp.zeros((32, HEAD_DIM), F32)
        for r in range(4):
            acc += dot_nn(rounded[:, r * 128 : (r + 1) * 128], cache[r, 1, :, column])
        dp_send[pl.ds(2 * k, 2), 0] = acc.reshape(2, 16, HEAD_DIM)
        dp_send[pl.ds(2 * k, 2), 1] = jnp.where(left, top, total).reshape(2, 16, HEAD_DIM)
        return carry

    lax.fori_loop(0, 4, decode_cached, 0)
    for step in (1, 3, 2):
        q_copy(step).wait_recv()
        q_forward(step).start()
    for step in range(1, 8):
        sa_copy(step).start()
    lax.fori_loop(4, 8, decode_cached, 0)

    local_kv.wait()
    offset = off_ref[0]

    def load_queries(slot):
        block = q_all[slot]
        return jnp.concatenate(
            [block[:, h * HEAD_DIM : (h + 1) * HEAD_DIM] for h in range(4)], axis=0
        )

    def attend(slots, queries, top):
        for b in slots:
            start = (c * 16 + kv_peer(b, -1)) * 256
            part = dot_nt(kv[b, 0], queries)
            part = jnp.where(start + iota((256, 256), 0) < offset, part, NEG)
            scores[b] = part
            top = jnp.maximum(top, jnp.max(part.reshape(32, 8, 256), axis=0))
        return jnp.max(top, axis=0, keepdims=True)

    def collect(slots, top, total, acc):
        for b in slots:
            weights = jnp.exp2((scores[b] - top) * EXP2_SCALE)
            total += jnp.sum(weights.reshape(32, 8, 256), axis=0)
            acc += dot_nn(vt[:, b * 256 : (b + 1) * 256], weights.astype(BF16))
        return total, acc

    def transpose_values(slots):
        for slot in slots:
            vt[:, slot * 256 : (slot + 1) * 256] = kv[slot, 1].astype(F32).T.astype(BF16)

    for slot in NEAR[1:]:
        kv_copy(slot).wait_recv()
    transpose_values(NEAR)

    def first_pass(i, carry):
        slot = (i + 1) % 8

        @pl.when(slot % 2 == 1)
        def _():
            q_forward(slot // 2).wait_recv()

        queries = load_queries(slot)
        top = attend(NEAR, queries, jnp.full((8, 256), NEG, F32))
        total, acc = collect(
            NEAR, top, jnp.zeros((8, 256), F32), jnp.zeros((HEAD_DIM, 256), F32)
        )
        run_top[slot] = jnp.broadcast_to(top, (8, 256))
        run_total[slot] = total
        run_acc[slot] = acc
        return carry

    lax.fori_loop(0, 8, first_pass, 0)

    for slot in range(1, 8):
        sp_copy(slot).wait_recv()
    for slot in FAR:
        kv_copy(slot).wait_recv()
    transpose_values(FAR)
    span_rows = sp_pre[...].reshape(64, HEAD_DIM)
    span_keys = span_rows.astype(BF16)
    span_vt = pltpu.roll(span_rows, 60, axis=0).T.astype(BF16)
    span_row = iota((64, 256), 0)
    span_slot = span_row // 8
    span_y = (y - span_slot // 2 + 4) % 4
    span_x = x + (span_slot % 2) * (3 - 2 * x)
    span_token = (c * 16 + span_y * 4 + span_x) * 4 + span_row % 8
    span_real = span_row % 8 < 4

    def second_pass(i, carry):
        slot = (i + 1) % 8
        far_c, _ = q_peer(slot, -1)
        queries = load_queries(slot)
        span_live = span_real & (span_token <= far_c * 64 + iota((64, 256), 1) % 64)
        span_part = jnp.where(span_live, dot_nt(span_keys, queries), NEG)
        top = jnp.max(span_part.reshape(8, 8, 256), axis=0)
        top = attend(FAR, queries, jnp.maximum(top, run_top[slot]))
        factor = jnp.exp2((run_top[slot] - top) * EXP2_SCALE)
        weights = jnp.where(span_live, jnp.exp2((span_part - top) * EXP2_SCALE), 0.0)
        total = run_total[slot] * factor + jnp.sum(weights.reshape(8, 8, 256), axis=0)
        acc = run_acc[slot] * factor[0:1] + dot_nn(span_vt, weights.astype(BF16))
        total, acc = collect(FAR, top, total, acc)
        total = jnp.sum(total, axis=0, keepdims=True)
        po_send[slot] = acc.astype(BF16)
        ps_send[slot] = jnp.where(iota((8, 256), 0) < 4, top, total)

        @pl.when(slot > 0)
        def _():
            po_copy(slot).start()
            ps_copy(slot).start()

        return carry

    lax.fori_loop(0, 8, second_pass, 0)

    for step in range(1, 8):
        sa_copy(step).wait_recv()
    sa_forward().start()
    sa_forward().wait_recv()
    sp_wide[...] = sp_all[...].reshape(16, 64, HEAD_DIM).astype(F32)
    new_col = iota((32, 128), 1)
    new_owner = select4(new_col // 32, [own_ref[r] for r in range(4)])
    new_row = (s * 4 + c) * 4 + iota((32, 128), 0) % 4
    new_live = (new_owner == new_row) & (new_col % 8 < 4)

    def decode_fresh(k, carry):
        queries = dq_all[pl.ds(2 * k, 2)].reshape(32, HEAD_DIM)
        fresh = (
            sp_wide[:, pl.ds(pl.multiple_of(8 * k, 8), 8), :].reshape(128, HEAD_DIM).astype(BF16)
        )
        stats = dp_send[pl.ds(2 * k, 2), 1].reshape(32, HEAD_DIM)
        former = stats[:, 0:1]
        part = jnp.where(new_live, dot_nt(queries, fresh), NEG)
        top = jnp.maximum(former, jnp.max(part, axis=1, keepdims=True))
        factor = jnp.exp2((former - top) * EXP2_SCALE)
        part = jnp.where(new_live, jnp.exp2((part - top) * EXP2_SCALE), 0.0)
        total = stats[:, 64:65] * factor + jnp.sum(part, axis=1, keepdims=True)
        acc = dp_send[pl.ds(2 * k, 2), 0].reshape(32, HEAD_DIM) * factor
        acc += dot_nn(pltpu.roll(part, 4, axis=1).astype(BF16), fresh)
        dp_send[pl.ds(2 * k, 2), 0] = acc.reshape(2, 16, HEAD_DIM)
        dp_send[pl.ds(2 * k, 2), 1] = jnp.where(left, top, total).reshape(2, 16, HEAD_DIM)
        return carry

    lax.fori_loop(0, 8, decode_fresh, 0)
    for step in range(1, 16):
        dp_copy(step).start()

    for step in range(1, 16):
        dp_copy(step).wait_recv()
    dp_recv[0] = dp_send[t]
    tops = [dp_recv[i, 1][:, 0:1] for i in range(16)]
    top = tops[0]
    for i in range(1, 16):
        top = jnp.maximum(top, tops[i])
    acc = jnp.zeros((16, HEAD_DIM), F32)
    total = jnp.zeros((16, 1), F32)
    for i in range(16):
        factor = jnp.exp2((tops[i] - top) * EXP2_SCALE)
        acc += dp_recv[i, 0] * factor
        total += dp_recv[i, 1][:, 64:65] * factor
    d_result[...] = acc / total
    for h in range(4):
        dout_ref[:, h * HEAD_DIM : (h + 1) * HEAD_DIM] = d_result[4 * h : 4 * h + 4, :].astype(BF16)

    for slot in range(1, 8):
        ps_copy(slot).wait_recv()
        po_copy(slot).wait_recv()
    ps_recv[0] = ps_send[0]
    po_recv[0] = po_send[0]
    top = ps_recv[0, 0:1, :]
    for i in range(1, 8):
        top = jnp.maximum(top, ps_recv[i, 0:1, :])
    acc = jnp.zeros((HEAD_DIM, 256), F32)
    total = jnp.zeros((1, 256), F32)
    for i in range(8):
        factor = jnp.exp2((ps_recv[i, 0:1, :] - top) * EXP2_SCALE)
        acc += po_recv[i].astype(F32) * factor
        total += ps_recv[i, 4:5, :] * factor
    result = (acc / total).T
    for h in range(4):
        out_ref[0, :, h * HEAD_DIM : (h + 1) * HEAD_DIM] = result[h * 64 : (h + 1) * 64].astype(BF16)

    for step in range(1, 16):
        dq_copy(step).wait_send()
        dp_copy(step).wait_send()
    for step in range(4):
        q_forward(step).wait_send()
    for step in range(1, 4):
        q_copy(step).wait_send()
    for step in range(1, 8):
        sa_copy(step).wait_send()
    sa_forward().wait_send()
    for slot in range(1, 8):
        kv_copy(slot).wait_send()
        sp_copy(slot).wait_send()
        po_copy(slot).wait_send()
        ps_copy(slot).wait_send()


def body(
    span_queries,
    prompt_cache,
    span_kv,
    span_offsets,
    decode_queries,
    decode_cache,
    cache_lengths,
    owner_rows,
):
    vmem = pl.BlockSpec(memory_space=pltpu.VMEM)
    hbm = pl.BlockSpec(memory_space=pltpu.HBM)
    sem = pltpu.SemaphoreType.DMA
    return pl.pallas_call(
        kernel,
        out_shape=(
            pltpu.VMEM(span_queries.shape, BF16),
            pltpu.VMEM(decode_queries.shape, BF16),
        ),
        in_specs=[hbm] * 8,
        out_specs=(vmem, vmem),
        scratch_shapes=[
            pltpu.SMEM((1,), jnp.int32),
            pltpu.SMEM((4,), jnp.int32),
            pltpu.SMEM((4,), jnp.int32),
            pltpu.VMEM((4, 512), BF16),
            pltpu.VMEM((1, 2, 4, 1024), BF16),
            pltpu.VMEM((4, 2, 128, 1024), BF16),
            pltpu.VMEM((8, 2, 256, HEAD_DIM), BF16),
            pltpu.VMEM((HEAD_DIM, 2048), BF16),
            pltpu.VMEM((8, 64, 512), BF16),
            pltpu.VMEM((8, 256, 256), F32),
            pltpu.VMEM((8, 8, 256), F32),
            pltpu.VMEM((8, 8, 256), F32),
            pltpu.VMEM((8, HEAD_DIM, 256), F32),
            pltpu.VMEM((8, HEAD_DIM, 256), BF16),
            pltpu.VMEM((8, HEAD_DIM, 256), BF16),
            pltpu.VMEM((8, 8, 256), F32),
            pltpu.VMEM((8, 8, 256), F32),
            pltpu.VMEM((8, 8, HEAD_DIM), F32),
            pltpu.VMEM((8, 8, HEAD_DIM), F32),
            pltpu.VMEM((64, HEAD_DIM), BF16),
            pltpu.VMEM((2, 2, 4, 64, HEAD_DIM), BF16),
            pltpu.VMEM((16, 64, HEAD_DIM), F32),
            pltpu.VMEM((16, HEAD_DIM), F32),
            pltpu.VMEM((16, HEAD_DIM), BF16),
            pltpu.VMEM((16, 16, HEAD_DIM), BF16),
            pltpu.VMEM((16, 2, 16, HEAD_DIM), F32),
            pltpu.VMEM((16, 2, 16, HEAD_DIM), F32),
            pltpu.VMEM((16, HEAD_DIM), F32),
            sem((8,)),
            sem((8,)),
            sem((8,)),
            sem((8,)),
            sem((8,)),
            sem((8,)),
            sem((8,)),
            sem((16,)),
            sem((16,)),
            sem((16,)),
            sem((16,)),
            sem((16,)),
            sem((16,)),
            sem((8,)),
            sem((8,)),
            sem((8,)),
            sem((8,)),
        ],
        compiler_params=pltpu.CompilerParams(
            collective_id=0, has_side_effects=True, vmem_limit_bytes=60 * 1024 * 1024
        ),
    )(
        span_offsets,
        cache_lengths,
        owner_rows,
        decode_queries,
        span_kv,
        span_queries,
        prompt_cache,
        decode_cache,
    )


def solution(mesh):
    return jax.shard_map(
        body,
        mesh=mesh,
        in_specs=(
            P("sect", "ctx", "tp"),
            P("sect", None, ("ctx", "tp"), None),
            P("sect", None, ("ctx", "tp"), None),
            P("sect"),
            P(("sect", "ctx"), "tp"),
            P(("sect", "ctx"), None, "tp", None),
            P(("sect", "ctx")),
            P(),
        ),
        out_specs=(P("sect", "ctx", "tp"), P(("sect", "ctx"), "tp")),
        check_vma=False,
    )
```

```python
import math

import jax
import jax.numpy as jnp
from jax import lax
from jax.experimental import pallas as pl
from jax.experimental.pallas import tpu as pltpu
from jax.sharding import PartitionSpec as P

HEAD_DIM = 128
MESH = pl.DeviceIdType.MESH
NEG = -1e30
EXP2_SCALE = math.log2(math.e) / math.sqrt(HEAD_DIM)
F32 = jnp.float32
BF16 = jnp.bfloat16
NEAR = (0, 1, 2, 6, 3, 7)
FAR = (4, 5)


def dot_nt(a, b):
    return lax.dot_general(a, b, (((1,), (1,)), ((), ())), preferred_element_type=F32)


def dot_nn(a, b):
    return lax.dot_general(a, b, (((1,), (0,)), ((), ())), preferred_element_type=F32)


def iota(shape, dim):
    return lax.broadcasted_iota(jnp.int32, shape, dim)


def select4(index, values):
    return jnp.where(
        index == 0,
        values[0],
        jnp.where(index == 1, values[1], jnp.where(index == 2, values[2], values[3])),
    )


def kernel(
    off_hbm,
    len_hbm,
    own_hbm,
    dq_hbm,
    skv_hbm,
    q_hbm,
    pc_hbm,
    dc_hbm,
    out_ref,
    dout_ref,
    off_ref,
    len_ref,
    own_ref,
    dq_ref,
    skv_ref,
    cache,
    staged,
    kv,
    vt,
    q_all,
    scores,
    run_top,
    run_total,
    run_acc,
    po_send,
    po_recv,
    ps_send,
    ps_recv,
    sp_head,
    sp_pre,
    sp_block,
    sp_all,
    sp_wide,
    dq_wide,
    dq_block,
    dq_all,
    dp_send,
    dp_recv,
    d_result,
    local_sem,
    stage_sem,
    kv_ssem,
    kv_rsem,
    q_ssem,
    q_rsem,
    sp_ssem,
    sp_rsem,
    sa_ssem,
    sa_rsem,
    ring_ssem,
    ring_rsem,
    dq_ssem,
    dq_rsem,
    dp_ssem,
    dp_rsem,
    po_ssem,
    po_rsem,
    ps_ssem,
    ps_rsem,
):
    s = lax.axis_index("sect")
    c = lax.axis_index("ctx")
    t = lax.axis_index("tp")
    y = t // 4
    x = t % 4
    head = t // 2
    pair = t + 1 - 2 * (t % 2)

    def kv_peer(slot, sign):
        a, b = slot // 2, slot % 2
        far_y = (y + sign * a + 4) % 4
        far_x = x + b * (3 - 2 * x)
        return far_y * 4 + far_x

    def q_peer(slot, sign):
        a, b = slot // 2, slot % 2
        return (c + sign * a + 4) % 4, t + b * (pair - t)

    core = s % 2
    layer = (s // 2) * 4 + c

    def kv_copy(slot):
        far = kv_peer(slot, 1)
        return pltpu.make_async_remote_copy(
            src_ref=staged.at[far // 2],
            dst_ref=kv.at[slot],
            send_sem=kv_ssem.at[slot],
            recv_sem=kv_rsem.at[slot],
            device_id=(s, c, far),
            device_id_type=MESH,
        )

    def q_copy(step):
        return pltpu.make_async_remote_copy(
            src_ref=q_all.at[0],
            dst_ref=q_all.at[2 * step],
            send_sem=q_ssem.at[2 * step],
            recv_sem=q_rsem.at[2 * step],
            device_id=(s, (c + step) % 4, t),
            device_id_type=MESH,
        )

    def q_forward(step):
        return pltpu.make_async_remote_copy(
            src_ref=q_all.at[2 * step],
            dst_ref=q_all.at[2 * step + 1],
            send_sem=q_ssem.at[2 * step + 1],
            recv_sem=q_rsem.at[2 * step + 1],
            device_id=(s, c, pair),
            device_id_type=MESH,
        )

    def sp_copy(slot):
        far = kv_peer(slot, 1)
        return pltpu.make_async_remote_copy(
            src_ref=sp_head.at[far // 2],
            dst_ref=sp_pre.at[slot],
            send_sem=sp_ssem.at[slot],
            recv_sem=sp_rsem.at[slot],
            device_id=(s, c, far),
            device_id_type=MESH,
        )

    def ring_peer(shift):
        far = (layer + shift + 8) % 8
        return (far // 4) * 2 + core, far % 4

    ring_steps = (((0, 1), (0, -1), (0, 2), (0, -2)), ((1, -2), (2, -2), (-1, 2)))

    def ring_copies(step):
        for index, (block, shift) in enumerate(ring_steps[step]):
            far_s, far_c = ring_peer(shift)
            moved = (layer + block + 8) % 8
            yield pltpu.make_async_remote_copy(
                src_ref=sp_all.at[moved // 4, core, moved % 4],
                dst_ref=sp_all.at[moved // 4, core, moved % 4],
                send_sem=ring_ssem.at[4 * step + index],
                recv_sem=ring_rsem.at[4 * step + index],
                device_id=(far_s, far_c, t),
                device_id_type=MESH,
            )

    def ring_start(step):
        for copy in ring_copies(step):
            copy.start()

    def ring_wait(step):
        for copy in ring_copies(step):
            copy.wait_recv()

    def sa_forward():
        return pltpu.make_async_remote_copy(
            src_ref=sp_all.at[:, core],
            dst_ref=sp_all.at[:, core],
            send_sem=sa_ssem,
            recv_sem=sa_rsem,
            device_id=(s + 1 - 2 * core, c, t),
            device_id_type=MESH,
        )

    def dq_copy(step):
        return pltpu.make_async_remote_copy(
            src_ref=dq_block,
            dst_ref=dq_all.at[t],
            send_sem=dq_ssem.at[step],
            recv_sem=dq_rsem.at[step],
            device_id=(s, c, (t + step) % 16),
            device_id_type=MESH,
        )

    def dp_copy(step):
        far = (t + step) % 16
        return pltpu.make_async_remote_copy(
            src_ref=dp_send.at[far],
            dst_ref=dp_recv.at[step],
            send_sem=dp_ssem.at[step],
            recv_sem=dp_rsem.at[step],
            device_id=(s, c, far),
            device_id_type=MESH,
        )

    def sum_peer(slot):
        far_c, far_t = q_peer(slot, -1)
        return jnp.where(slot == 5, c, far_c), far_t

    def po_copy(slot):
        far_c, far_t = sum_peer(slot)
        return pltpu.make_async_remote_copy(
            src_ref=po_send.at[slot],
            dst_ref=po_recv.at[slot],
            send_sem=po_ssem.at[slot],
            recv_sem=po_rsem.at[slot],
            device_id=(s, far_c, far_t),
            device_id_type=MESH,
        )

    def ps_copy(slot):
        far_c, far_t = sum_peer(slot)
        return pltpu.make_async_remote_copy(
            src_ref=ps_send.at[slot],
            dst_ref=ps_recv.at[slot],
            send_sem=ps_ssem.at[slot],
            recv_sem=ps_rsem.at[slot],
            device_id=(s, far_c, far_t),
            device_id_type=MESH,
        )

    barrier = pltpu.get_barrier_semaphore()

    def greet(far_s, far_c, far_t):
        pl.semaphore_signal(
            barrier, inc=1, device_id=(far_s, far_c, far_t), device_id_type=MESH
        )

    for shift in (2, -2, 1, -1):
        far_s, far_c = ring_peer(shift)
        greet(far_s, far_c, t)
    for step in range(1, 16):
        greet(s, c, (t + step) % 16)
    for step in range(1, 4):
        greet(s, (c + step) % 4, t)
        greet(s, (c + step) % 4, pair)
    greet(s + 1 - 2 * core, c, t)

    own_column = pl.multiple_of(head * HEAD_DIM, HEAD_DIM)
    local_small = [
        pltpu.make_async_copy(source, target, local_sem.at[3 + i])
        for i, (source, target) in enumerate(
            [
                (dq_hbm, dq_ref),
                (skv_hbm, skv_ref),
                (off_hbm, off_ref),
                (len_hbm, len_ref),
                (own_hbm, own_ref),
            ]
        )
    ]
    for copy in local_small:
        copy.start()
    local_kv = pltpu.make_async_copy(
        pc_hbm.at[0, :, :, pl.ds(own_column, HEAD_DIM)], kv.at[0], local_sem.at[0]
    )
    local_q = pltpu.make_async_copy(q_hbm.at[0], q_all.at[0], local_sem.at[1])
    local_cache = pltpu.make_async_copy(dc_hbm, cache, local_sem.at[2])
    local_q.start()
    stage = [
        pltpu.make_async_copy(
            pc_hbm.at[0, :, :, h * HEAD_DIM : (h + 1) * HEAD_DIM], staged.at[h], stage_sem.at[h]
        )
        for h in range(8)
    ]
    for copy in stage:
        copy.start()
    local_kv.start()
    local_cache.start()

    for copy in local_small:
        copy.wait()
    own_q = dq_ref[...].astype(F32)
    span_k = skv_ref[0, 0].astype(F32)
    span_v = skv_ref[0, 1].astype(F32)
    for h in range(4):
        dq_wide[4 * h : 4 * h + 4, :] = own_q[:, h * HEAD_DIM : (h + 1) * HEAD_DIM]
    for h in range(8):
        sp_head[h, 0:4, :] = span_k[:, h * HEAD_DIM : (h + 1) * HEAD_DIM]
        sp_head[h, 4:8, :] = span_v[:, h * HEAD_DIM : (h + 1) * HEAD_DIM]
    dq_block[...] = dq_wide[...].astype(BF16)
    sp_block[...] = sp_head[...].reshape(64, HEAD_DIM).astype(BF16)
    dq_all[t] = dq_block[...]
    sp_all[s // 2, core, c] = sp_block[...]
    sp_pre[0] = sp_head[head]
    local_q.wait()
    for copy in stage:
        copy.wait()

    pl.semaphore_wait(barrier, 26)

    for step in range(1, 16):
        dq_copy(step).start()
    ring_start(0)
    for slot in NEAR[1:]:
        kv_copy(slot).start()
    q_forward(0).start()
    for step in range(1, 4):
        q_copy(step).start()
    for slot in FAR:
        kv_copy(slot).start()
    for slot in range(1, 8):
        sp_copy(slot).start()

    local_cache.wait()
    for step in range(1, 16):
        dq_copy(step).wait_recv()
    row_q = iota((32, 512), 0) % 4
    row_p = iota((32, 512), 1) // 128
    pos = t * 128 + iota((32, 512), 1) % 128
    length = select4(row_p, [len_ref[r] for r in range(4)])
    cache_live = (row_q == row_p) & (pos < length)
    left = iota((32, 128), 1) < 64

    def decode_cached(k, carry):
        column = pl.ds(pl.multiple_of(k * HEAD_DIM, HEAD_DIM), HEAD_DIM)
        queries = dq_all[pl.ds(2 * k, 2)].reshape(32, HEAD_DIM)
        part = jnp.concatenate(
            [dot_nt(queries, cache[r, 0, :, column]) for r in range(4)], axis=1
        )
        part = jnp.where(cache_live, part, NEG)
        top = jnp.max(part, axis=1, keepdims=True)
        part = jnp.exp2((part - top) * EXP2_SCALE)
        total = jnp.sum(part, axis=1, keepdims=True)
        rounded = part.astype(BF16)
        acc = jnp.zeros((32, HEAD_DIM), F32)
        for r in range(4):
            acc += dot_nn(rounded[:, r * 128 : (r + 1) * 128], cache[r, 1, :, column])
        dp_send[pl.ds(2 * k, 2), 0] = acc.reshape(2, 16, HEAD_DIM)
        dp_send[pl.ds(2 * k, 2), 1] = jnp.where(left, top, total).reshape(2, 16, HEAD_DIM)
        return carry

    lax.fori_loop(0, 4, decode_cached, 0)
    for step in (1, 3):
        q_copy(step).wait_recv()
        q_forward(step).start()
    lax.fori_loop(4, 8, decode_cached, 0)
    q_copy(2).wait_recv()
    q_forward(2).start()
    ring_wait(0)
    ring_start(1)

    local_kv.wait()
    offset = off_ref[0]

    def load_queries(slot):
        block = q_all[slot]
        return jnp.concatenate(
            [block[:, h * HEAD_DIM : (h + 1) * HEAD_DIM] for h in range(4)], axis=0
        )

    def attend(slots, queries, top):
        for b in slots:
            start = (c * 16 + kv_peer(b, -1)) * 256
            part = dot_nt(kv[b, 0], queries)
            part = jnp.where(start + iota((256, 256), 0) < offset, part, NEG)
            scores[b] = part
            top = jnp.maximum(top, jnp.max(part.reshape(32, 8, 256), axis=0))
        return jnp.max(top, axis=0, keepdims=True)

    def collect(slots, top, total, acc):
        for b in slots:
            weights = jnp.exp2((scores[b] - top) * EXP2_SCALE)
            total += jnp.sum(weights.reshape(32, 8, 256), axis=0)
            acc += dot_nn(vt[:, b * 256 : (b + 1) * 256], weights.astype(BF16))
        return total, acc

    def transpose_values(slots):
        for slot in slots:
            vt[:, slot * 256 : (slot + 1) * 256] = kv[slot, 1].astype(F32).T.astype(BF16)

    for slot in NEAR[1:]:
        kv_copy(slot).wait_recv()
    transpose_values(NEAR)

    def first_pass(i, carry):
        slot = (2 * i) % 8 + i // 4

        @pl.when(slot % 2 == 1)
        def _():
            q_forward(slot // 2).wait_recv()

        queries = load_queries(slot)
        top = attend(NEAR, queries, jnp.full((8, 256), NEG, F32))
        total, acc = collect(
            NEAR, top, jnp.zeros((8, 256), F32), jnp.zeros((HEAD_DIM, 256), F32)
        )
        run_top[slot] = jnp.broadcast_to(top, (8, 256))
        run_total[slot] = total
        run_acc[slot] = acc
        return carry

    lax.fori_loop(0, 4, first_pass, 0)
    ring_wait(1)
    sa_forward().start()
    lax.fori_loop(4, 8, first_pass, 0)

    for slot in range(1, 8):
        sp_copy(slot).wait_recv()
    for slot in FAR:
        kv_copy(slot).wait_recv()
    transpose_values(FAR)
    span_rows = sp_pre[...].reshape(64, HEAD_DIM)
    span_keys = span_rows.astype(BF16)
    span_vt = pltpu.roll(span_rows, 60, axis=0).T.astype(BF16)
    span_row = iota((64, 256), 0)
    span_slot = span_row // 8
    span_y = (y - span_slot // 2 + 4) % 4
    span_x = x + (span_slot % 2) * (3 - 2 * x)
    span_token = (c * 16 + span_y * 4 + span_x) * 4 + span_row % 8
    span_real = span_row % 8 < 4

    def publish(slot, top, total, acc):
        po_send[slot] = acc.astype(BF16)
        ps_send[slot] = jnp.where(iota((8, 256), 0) < 4, top, total)

    def second_pass(i, carry):
        slot = (i + 5) % 8
        far_c, _ = q_peer(slot, -1)
        queries = load_queries(slot)
        span_live = span_real & (span_token <= far_c * 64 + iota((64, 256), 1) % 64)
        span_part = jnp.where(span_live, dot_nt(span_keys, queries), NEG)
        top = jnp.max(span_part.reshape(8, 8, 256), axis=0)
        top = attend(FAR, queries, jnp.maximum(top, run_top[slot]))
        factor = jnp.exp2((run_top[slot] - top) * EXP2_SCALE)
        weights = jnp.where(span_live, jnp.exp2((span_part - top) * EXP2_SCALE), 0.0)
        total = run_total[slot] * factor + jnp.sum(weights.reshape(8, 8, 256), axis=0)
        acc = run_acc[slot] * factor[0:1] + dot_nn(span_vt, weights.astype(BF16))
        total, acc = collect(FAR, top, total, acc)
        total = jnp.sum(total, axis=0, keepdims=True)

        @pl.when(slot != 4)
        def _():
            publish(slot, top, total, acc)

        @pl.when((slot != 0) & (slot != 4))
        def _():
            po_copy(slot).start()
            ps_copy(slot).start()

        @pl.when(slot == 4)
        def _():
            run_top[4] = jnp.broadcast_to(top, (8, 256))
            run_total[4] = jnp.broadcast_to(total, (8, 256))
            run_acc[4] = acc

        return carry

    lax.fori_loop(0, 8, second_pass, 0)

    def join(one, other):
        top = jnp.maximum(one[0], other[0])
        left = jnp.exp2((one[0] - top) * EXP2_SCALE)
        right = jnp.exp2((other[0] - top) * EXP2_SCALE)
        return top, one[1] * left + other[1] * right, one[2] * left + other[2] * right

    def received(slot):
        po_copy(slot).wait_recv()
        ps_copy(slot).wait_recv()
        return ps_recv[slot, 0:1, :], ps_recv[slot, 4:5, :], po_recv[slot].astype(F32)

    sa_forward().wait_recv()
    sp_wide[...] = sp_all[...].reshape(16, 64, HEAD_DIM).astype(F32)
    new_col = iota((32, 128), 1)
    new_owner = select4(new_col // 32, [own_ref[r] for r in range(4)])
    new_row = (s * 4 + c) * 4 + iota((32, 128), 0) % 4
    new_live = (new_owner == new_row) & (new_col % 8 < 4)

    def decode_fresh(k, carry):
        queries = dq_all[pl.ds(2 * k, 2)].reshape(32, HEAD_DIM)
        fresh = (
            sp_wide[:, pl.ds(pl.multiple_of(8 * k, 8), 8), :].reshape(128, HEAD_DIM).astype(BF16)
        )
        stats = dp_send[pl.ds(2 * k, 2), 1].reshape(32, HEAD_DIM)
        former = stats[:, 0:1]
        part = jnp.where(new_live, dot_nt(queries, fresh), NEG)
        top = jnp.maximum(former, jnp.max(part, axis=1, keepdims=True))
        factor = jnp.exp2((former - top) * EXP2_SCALE)
        part = jnp.where(new_live, jnp.exp2((part - top) * EXP2_SCALE), 0.0)
        total = stats[:, 64:65] * factor + jnp.sum(part, axis=1, keepdims=True)
        acc = dp_send[pl.ds(2 * k, 2), 0].reshape(32, HEAD_DIM) * factor
        acc += dot_nn(pltpu.roll(part, 4, axis=1).astype(BF16), fresh)
        dp_send[pl.ds(2 * k, 2), 0] = acc.reshape(2, 16, HEAD_DIM)
        dp_send[pl.ds(2 * k, 2), 1] = jnp.where(left, top, total).reshape(2, 16, HEAD_DIM)
        return carry

    lax.fori_loop(0, 8, decode_fresh, 0)
    for step in range(1, 16):
        dp_copy(step).start()

    publish(4, *join((run_top[4, 0:1, :], run_total[4, 0:1, :], run_acc[4]), received(5)))
    po_copy(4).start()
    ps_copy(4).start()

    state = (ps_send[0, 0:1, :], ps_send[0, 4:5, :], po_send[0].astype(F32))
    for slot in (1, 6, 7, 2, 3):
        state = join(state, received(slot))

    for step in range(1, 16):
        dp_copy(step).wait_recv()
    dp_recv[0] = dp_send[t]
    tops = [dp_recv[i, 1][:, 0:1] for i in range(16)]
    top = tops[0]
    for i in range(1, 16):
        top = jnp.maximum(top, tops[i])
    acc = jnp.zeros((16, HEAD_DIM), F32)
    total = jnp.zeros((16, 1), F32)
    for i in range(16):
        factor = jnp.exp2((tops[i] - top) * EXP2_SCALE)
        acc += dp_recv[i, 0] * factor
        total += dp_recv[i, 1][:, 64:65] * factor
    d_result[...] = acc / total
    for h in range(4):
        dout_ref[:, h * HEAD_DIM : (h + 1) * HEAD_DIM] = d_result[4 * h : 4 * h + 4, :].astype(BF16)

    _, total, acc = join(state, received(4))
    result = (acc / total).T
    for h in range(4):
        out_ref[0, :, h * HEAD_DIM : (h + 1) * HEAD_DIM] = result[h * 64 : (h + 1) * 64].astype(BF16)

    for step in range(1, 16):
        dq_copy(step).wait_send()
        dp_copy(step).wait_send()
    for step in range(4):
        q_forward(step).wait_send()
    for step in range(1, 4):
        q_copy(step).wait_send()
    for step in range(2):
        for copy in ring_copies(step):
            copy.wait_send()
    sa_forward().wait_send()
    for slot in range(1, 8):
        kv_copy(slot).wait_send()
        sp_copy(slot).wait_send()
        po_copy(slot).wait_send()
        ps_copy(slot).wait_send()


def body(
    span_queries,
    prompt_cache,
    span_kv,
    span_offsets,
    decode_queries,
    decode_cache,
    cache_lengths,
    owner_rows,
):
    vmem = pl.BlockSpec(memory_space=pltpu.VMEM)
    hbm = pl.BlockSpec(memory_space=pltpu.HBM)
    sem = pltpu.SemaphoreType.DMA
    return pl.pallas_call(
        kernel,
        out_shape=(
            pltpu.VMEM(span_queries.shape, BF16),
            pltpu.VMEM(decode_queries.shape, BF16),
        ),
        in_specs=[hbm] * 8,
        out_specs=(vmem, vmem),
        scratch_shapes=[
            pltpu.SMEM((1,), jnp.int32),
            pltpu.SMEM((4,), jnp.int32),
            pltpu.SMEM((4,), jnp.int32),
            pltpu.VMEM((4, 512), BF16),
            pltpu.VMEM((1, 2, 4, 1024), BF16),
            pltpu.VMEM((4, 2, 128, 1024), BF16),
            pltpu.VMEM((8, 2, 256, HEAD_DIM), BF16),
            pltpu.VMEM((8, 2, 256, HEAD_DIM), BF16),
            pltpu.VMEM((HEAD_DIM, 2048), BF16),
            pltpu.VMEM((8, 64, 512), BF16),
            pltpu.VMEM((8, 256, 256), F32),
            pltpu.VMEM((8, 8, 256), F32),
            pltpu.VMEM((8, 8, 256), F32),
            pltpu.VMEM((8, HEAD_DIM, 256), F32),
            pltpu.VMEM((8, HEAD_DIM, 256), BF16),
            pltpu.VMEM((8, HEAD_DIM, 256), BF16),
            pltpu.VMEM((8, 8, 256), F32),
            pltpu.VMEM((8, 8, 256), F32),
            pltpu.VMEM((8, 8, HEAD_DIM), F32),
            pltpu.VMEM((8, 8, HEAD_DIM), F32),
            pltpu.VMEM((64, HEAD_DIM), BF16),
            pltpu.VMEM((2, 2, 4, 64, HEAD_DIM), BF16),
            pltpu.VMEM((16, 64, HEAD_DIM), F32),
            pltpu.VMEM((16, HEAD_DIM), F32),
            pltpu.VMEM((16, HEAD_DIM), BF16),
            pltpu.VMEM((16, 16, HEAD_DIM), BF16),
            pltpu.VMEM((16, 2, 16, HEAD_DIM), F32),
            pltpu.VMEM((16, 2, 16, HEAD_DIM), F32),
            pltpu.VMEM((16, HEAD_DIM), F32),
            sem((8,)),
            sem((8,)),
            sem((8,)),
            sem((8,)),
            sem((8,)),
            sem((8,)),
            sem((8,)),
            sem((8,)),
            sem(()),
            sem(()),
            sem((8,)),
            sem((8,)),
            sem((16,)),
            sem((16,)),
            sem((16,)),
            sem((16,)),
            sem((8,)),
            sem((8,)),
            sem((8,)),
            sem((8,)),
        ],
        compiler_params=pltpu.CompilerParams(
            collective_id=0, has_side_effects=True, vmem_limit_bytes=60 * 1024 * 1024
        ),
    )(
        span_offsets,
        cache_lengths,
        owner_rows,
        decode_queries,
        span_kv,
        span_queries,
        prompt_cache,
        decode_cache,
    )


def solution(mesh):
    return jax.shard_map(
        body,
        mesh=mesh,
        in_specs=(
            P("sect", "ctx", "tp"),
            P("sect", None, ("ctx", "tp"), None),
            P("sect", None, ("ctx", "tp"), None),
            P("sect"),
            P(("sect", "ctx"), "tp"),
            P(("sect", "ctx"), None, "tp", None),
            P(("sect", "ctx")),
            P(),
        ),
        out_specs=(P("sect", "ctx", "tp"), P(("sect", "ctx"), "tp")),
        check_vma=False,
    )
```

```python
import math

import jax
import jax.numpy as jnp
from jax import lax
from jax.experimental import pallas as pl
from jax.experimental.pallas import tpu as pltpu
from jax.sharding import PartitionSpec as P

HEAD_DIM = 128
MESH = pl.DeviceIdType.MESH
NEG = -1e30
EXP2_SCALE = math.log2(math.e) / math.sqrt(HEAD_DIM)
F32 = jnp.float32
BF16 = jnp.bfloat16
NEAR = (0, 1, 2, 6, 3, 7)
FAR = (4, 5)


def dot_nt(a, b):
    return lax.dot_general(a, b, (((1,), (1,)), ((), ())), preferred_element_type=F32)


def dot_nn(a, b):
    return lax.dot_general(a, b, (((1,), (0,)), ((), ())), preferred_element_type=F32)


def iota(shape, dim):
    return lax.broadcasted_iota(jnp.int32, shape, dim)


def select4(index, values):
    return jnp.where(
        index == 0,
        values[0],
        jnp.where(index == 1, values[1], jnp.where(index == 2, values[2], values[3])),
    )


def kernel(
    off_hbm,
    len_hbm,
    own_hbm,
    dq_hbm,
    skv_hbm,
    q_hbm,
    pc_hbm,
    dc_hbm,
    out_ref,
    dout_ref,
    off_ref,
    len_ref,
    own_ref,
    dq_ref,
    skv_ref,
    cache,
    staged,
    kv,
    vt,
    q_all,
    scores,
    span_scores,
    run_top,
    run_total,
    run_acc,
    po_send,
    po_recv,
    ps_send,
    ps_recv,
    sp_head,
    sp_pre,
    sp_block,
    sp_all,
    sp_wide,
    dq_wide,
    dq_block,
    dq_all,
    dp_send,
    dp_recv,
    d_result,
    local_sem,
    stage_sem,
    kv_ssem,
    kv_rsem,
    q_ssem,
    q_rsem,
    sp_ssem,
    sp_rsem,
    sa_ssem,
    sa_rsem,
    ring_ssem,
    ring_rsem,
    dq_ssem,
    dq_rsem,
    dp_ssem,
    dp_rsem,
    po_ssem,
    po_rsem,
    ps_ssem,
    ps_rsem,
):
    s = lax.axis_index("sect")
    c = lax.axis_index("ctx")
    t = lax.axis_index("tp")
    y = t // 4
    x = t % 4
    head = t // 2
    pair = t + 1 - 2 * (t % 2)

    def kv_peer(slot, sign):
        a, b = slot // 2, slot % 2
        far_y = (y + sign * a + 4) % 4
        far_x = x + b * (3 - 2 * x)
        return far_y * 4 + far_x

    def q_peer(slot, sign):
        a, b = slot // 2, slot % 2
        return (c + sign * a + 4) % 4, t + b * (pair - t)

    core = s % 2
    layer = (s // 2) * 4 + c

    def kv_copy(slot):
        far = kv_peer(slot, 1)
        return pltpu.make_async_remote_copy(
            src_ref=staged.at[far // 2],
            dst_ref=kv.at[slot],
            send_sem=kv_ssem.at[slot],
            recv_sem=kv_rsem.at[slot],
            device_id=(s, c, far),
            device_id_type=MESH,
        )

    def q_copy(step):
        return pltpu.make_async_remote_copy(
            src_ref=q_all.at[0],
            dst_ref=q_all.at[2 * step],
            send_sem=q_ssem.at[2 * step],
            recv_sem=q_rsem.at[2 * step],
            device_id=(s, (c + step) % 4, t),
            device_id_type=MESH,
        )

    def q_forward(step):
        return pltpu.make_async_remote_copy(
            src_ref=q_all.at[2 * step],
            dst_ref=q_all.at[2 * step + 1],
            send_sem=q_ssem.at[2 * step + 1],
            recv_sem=q_rsem.at[2 * step + 1],
            device_id=(s, c, pair),
            device_id_type=MESH,
        )

    def sp_copy(slot):
        far = kv_peer(slot, 1)
        return pltpu.make_async_remote_copy(
            src_ref=sp_head.at[far // 2],
            dst_ref=sp_pre.at[slot],
            send_sem=sp_ssem.at[slot],
            recv_sem=sp_rsem.at[slot],
            device_id=(s, c, far),
            device_id_type=MESH,
        )

    def ring_peer(shift):
        far = (layer + shift + 8) % 8
        return (far // 4) * 2 + core, far % 4

    ring_steps = (((0, 1), (0, -1), (0, 2), (0, -2)), ((1, -2), (2, -2), (-1, 2)))

    def ring_copies(step):
        for index, (block, shift) in enumerate(ring_steps[step]):
            far_s, far_c = ring_peer(shift)
            moved = (layer + block + 8) % 8
            yield pltpu.make_async_remote_copy(
                src_ref=sp_all.at[moved // 4, core, moved % 4],
                dst_ref=sp_all.at[moved // 4, core, moved % 4],
                send_sem=ring_ssem.at[4 * step + index],
                recv_sem=ring_rsem.at[4 * step + index],
                device_id=(far_s, far_c, t),
                device_id_type=MESH,
            )

    def ring_start(step):
        for copy in ring_copies(step):
            copy.start()

    def ring_wait(step):
        for copy in ring_copies(step):
            copy.wait_recv()

    def sa_forward():
        return pltpu.make_async_remote_copy(
            src_ref=sp_all.at[:, core],
            dst_ref=sp_all.at[:, core],
            send_sem=sa_ssem,
            recv_sem=sa_rsem,
            device_id=(s + 1 - 2 * core, c, t),
            device_id_type=MESH,
        )

    def dq_copy(step):
        return pltpu.make_async_remote_copy(
            src_ref=dq_block,
            dst_ref=dq_all.at[t],
            send_sem=dq_ssem.at[step],
            recv_sem=dq_rsem.at[step],
            device_id=(s, c, (t + step) % 16),
            device_id_type=MESH,
        )

    def dp_copy(step):
        far = (t + step) % 16
        return pltpu.make_async_remote_copy(
            src_ref=dp_send.at[far],
            dst_ref=dp_recv.at[step],
            send_sem=dp_ssem.at[step],
            recv_sem=dp_rsem.at[step],
            device_id=(s, c, far),
            device_id_type=MESH,
        )

    def sum_peer(slot):
        far_c, far_t = q_peer(slot, -1)
        return jnp.where(slot == 5, c, far_c), far_t

    def po_copy(slot):
        far_c, far_t = sum_peer(slot)
        return pltpu.make_async_remote_copy(
            src_ref=po_send.at[slot],
            dst_ref=po_recv.at[slot],
            send_sem=po_ssem.at[slot],
            recv_sem=po_rsem.at[slot],
            device_id=(s, far_c, far_t),
            device_id_type=MESH,
        )

    def ps_copy(slot):
        far_c, far_t = sum_peer(slot)
        return pltpu.make_async_remote_copy(
            src_ref=ps_send.at[slot],
            dst_ref=ps_recv.at[slot],
            send_sem=ps_ssem.at[slot],
            recv_sem=ps_rsem.at[slot],
            device_id=(s, far_c, far_t),
            device_id_type=MESH,
        )

    barrier = pltpu.get_barrier_semaphore()

    def greet(far_s, far_c, far_t):
        pl.semaphore_signal(
            barrier, inc=1, device_id=(far_s, far_c, far_t), device_id_type=MESH
        )

    for shift in (2, -2, 1, -1):
        far_s, far_c = ring_peer(shift)
        greet(far_s, far_c, t)
    for step in range(1, 16):
        greet(s, c, (t + step) % 16)
    for step in range(1, 4):
        greet(s, (c + step) % 4, t)
        greet(s, (c + step) % 4, pair)
    greet(s + 1 - 2 * core, c, t)

    own_column = pl.multiple_of(head * HEAD_DIM, HEAD_DIM)
    local_small = [
        pltpu.make_async_copy(source, target, local_sem.at[3 + i])
        for i, (source, target) in enumerate(
            [
                (dq_hbm, dq_ref),
                (skv_hbm, skv_ref),
                (off_hbm, off_ref),
                (len_hbm, len_ref),
                (own_hbm, own_ref),
            ]
        )
    ]
    for copy in local_small:
        copy.start()
    local_kv = pltpu.make_async_copy(
        pc_hbm.at[0, :, :, pl.ds(own_column, HEAD_DIM)], kv.at[0], local_sem.at[0]
    )
    local_q = pltpu.make_async_copy(q_hbm.at[0], q_all.at[0], local_sem.at[1])
    local_cache = pltpu.make_async_copy(dc_hbm, cache, local_sem.at[2])
    local_q.start()
    stage = [
        pltpu.make_async_copy(
            pc_hbm.at[0, :, :, h * HEAD_DIM : (h + 1) * HEAD_DIM], staged.at[h], stage_sem.at[h]
        )
        for h in range(8)
    ]
    for copy in stage:
        copy.start()
    local_kv.start()
    local_cache.start()

    for copy in local_small:
        copy.wait()
    own_q = dq_ref[...].astype(F32)
    span_k = skv_ref[0, 0].astype(F32)
    span_v = skv_ref[0, 1].astype(F32)
    for h in range(4):
        dq_wide[4 * h : 4 * h + 4, :] = own_q[:, h * HEAD_DIM : (h + 1) * HEAD_DIM]
    for h in range(8):
        sp_head[h, 0:4, :] = span_k[:, h * HEAD_DIM : (h + 1) * HEAD_DIM]
        sp_head[h, 4:8, :] = span_v[:, h * HEAD_DIM : (h + 1) * HEAD_DIM]
    dq_block[...] = dq_wide[...].astype(BF16)
    sp_block[...] = sp_head[...].reshape(64, HEAD_DIM).astype(BF16)
    dq_all[t] = dq_block[...]
    sp_all[s // 2, core, c] = sp_block[...]
    sp_pre[0] = sp_head[head]
    local_q.wait()
    for copy in stage:
        copy.wait()

    pl.semaphore_wait(barrier, 26)

    for step in range(1, 16):
        dq_copy(step).start()
    ring_start(0)
    for slot in NEAR[1:]:
        kv_copy(slot).start()
    q_forward(0).start()
    for step in range(1, 4):
        q_copy(step).start()
    for slot in FAR:
        kv_copy(slot).start()
    for slot in range(1, 8):
        sp_copy(slot).start()

    local_cache.wait()
    for step in range(1, 16):
        dq_copy(step).wait_recv()
    row_q = iota((32, 512), 0) % 4
    row_p = iota((32, 512), 1) // 128
    pos = t * 128 + iota((32, 512), 1) % 128
    length = select4(row_p, [len_ref[r] for r in range(4)])
    cache_live = (row_q == row_p) & (pos < length)
    left = iota((32, 128), 1) < 64

    def decode_cached(k, carry):
        column = pl.ds(pl.multiple_of(k * HEAD_DIM, HEAD_DIM), HEAD_DIM)
        queries = dq_all[pl.ds(2 * k, 2)].reshape(32, HEAD_DIM)
        part = jnp.concatenate(
            [dot_nt(queries, cache[r, 0, :, column]) for r in range(4)], axis=1
        )
        part = jnp.where(cache_live, part, NEG)
        top = jnp.max(part, axis=1, keepdims=True)
        part = jnp.exp2((part - top) * EXP2_SCALE)
        total = jnp.sum(part, axis=1, keepdims=True)
        rounded = part.astype(BF16)
        acc = jnp.zeros((32, HEAD_DIM), F32)
        for r in range(4):
            acc += dot_nn(rounded[:, r * 128 : (r + 1) * 128], cache[r, 1, :, column])
        dp_send[pl.ds(2 * k, 2), 0] = acc.reshape(2, 16, HEAD_DIM)
        dp_send[pl.ds(2 * k, 2), 1] = jnp.where(left, top, total).reshape(2, 16, HEAD_DIM)
        return carry

    lax.fori_loop(0, 4, decode_cached, 0)
    for step in (1, 3):
        q_copy(step).wait_recv()
        q_forward(step).start()
    lax.fori_loop(4, 8, decode_cached, 0)
    q_copy(2).wait_recv()
    q_forward(2).start()
    ring_wait(0)
    ring_start(1)

    local_kv.wait()
    offset = off_ref[0]

    def load_queries(slot):
        block = q_all[slot]
        return jnp.concatenate(
            [block[:, h * HEAD_DIM : (h + 1) * HEAD_DIM] for h in range(4)], axis=0
        )

    def attend_block(b, queries, top, side):
        start = (c * 16 + kv_peer(b, -1)) * 256
        part = dot_nt(kv[b, 0], queries)
        part = jnp.where(start + iota((256, 256), 0) < offset, part, NEG)
        scores[side, b] = part
        return jnp.maximum(top, jnp.max(part.reshape(32, 8, 256), axis=0))

    def collect_block(b, top, total, acc, side):
        weights = jnp.exp2((scores[side, b] - top) * EXP2_SCALE)
        total += jnp.sum(weights.reshape(32, 8, 256), axis=0)
        acc += dot_nn(vt[:, b * 256 : (b + 1) * 256], weights.astype(BF16))
        return total, acc

    def transpose_values(slots):
        for slot in slots:
            vt[:, slot * 256 : (slot + 1) * 256] = kv[slot, 1].astype(F32).T.astype(BF16)

    for slot in NEAR[1:]:
        kv_copy(slot).wait_recv()
    transpose_values(NEAR)

    def first_queries(i):
        slot = (2 * i) % 8 + i // 4

        @pl.when(slot % 2 == 1)
        def _():
            q_forward(slot // 2).wait_recv()

        return load_queries(slot)

    def first_step(i, top, side, last=False):
        slot = (2 * i) % 8 + i // 4
        queries = None if last else first_queries(i + 1)
        total, acc = jnp.zeros((8, 256), F32), jnp.zeros((HEAD_DIM, 256), F32)
        later = jnp.full((8, 256), NEG, F32)
        for b in NEAR:
            if not last:
                later = attend_block(b, queries, later, 1 - side)
            total, acc = collect_block(b, top, total, acc, side)
        run_top[slot] = jnp.broadcast_to(top, (8, 256))
        run_total[slot] = total
        run_acc[slot] = acc
        return jnp.max(later, axis=0, keepdims=True)

    def first_steps(i, top):
        return first_step(2 * i + 1, first_step(2 * i, top, 0), 1)

    top = jnp.full((8, 256), NEG, F32)
    queries = load_queries(0)
    for b in NEAR:
        top = attend_block(b, queries, top, 0)
    top = jnp.max(top, axis=0, keepdims=True)
    top = lax.fori_loop(0, 2, first_steps, top)
    ring_wait(1)
    sa_forward().start()
    top = lax.fori_loop(2, 3, first_steps, top)
    top = first_step(6, top, 0)
    first_step(7, top, 1, last=True)

    for slot in range(1, 8):
        sp_copy(slot).wait_recv()
    for slot in FAR:
        kv_copy(slot).wait_recv()
    transpose_values(FAR)
    span_rows = sp_pre[...].reshape(64, HEAD_DIM)
    span_keys = span_rows.astype(BF16)
    span_vt = pltpu.roll(span_rows, 60, axis=0).T.astype(BF16)
    span_row = iota((64, 256), 0)
    span_slot = span_row // 8
    span_y = (y - span_slot // 2 + 4) % 4
    span_x = x + (span_slot % 2) * (3 - 2 * x)
    span_token = (c * 16 + span_y * 4 + span_x) * 4 + span_row % 8
    span_real = span_row % 8 < 4

    def publish(slot, top, total, acc):
        po_send[slot] = acc.astype(BF16)
        row = iota((8, HEAD_DIM), 0)
        tops = jnp.where(row % 2 == 0, top[:, :HEAD_DIM], top[:, HEAD_DIM:])
        totals = jnp.where(row % 2 == 0, total[:, :HEAD_DIM], total[:, HEAD_DIM:])
        ps_send[slot] = jnp.where(row < 2, tops, totals)

    def span_live_at(slot):
        far_c, _ = q_peer(slot, -1)
        return span_real & (span_token <= far_c * 64 + iota((64, 256), 1) % 64)

    def second_queries(i, side):
        slot = (i + 5) % 8
        queries = load_queries(slot)
        part = jnp.where(span_live_at(slot), dot_nt(span_keys, queries), NEG)
        span_scores[side] = part
        top = jnp.maximum(run_top[slot], jnp.max(part.reshape(8, 8, 256), axis=0))
        return queries, top

    def second_step(i, top, side, last=False):
        slot = (i + 5) % 8
        queries, later = (None, None) if last else second_queries(i + 1, 1 - side)
        factor = jnp.exp2((run_top[slot] - top) * EXP2_SCALE)
        weights = jnp.exp2((span_scores[side] - top) * EXP2_SCALE)
        weights = jnp.where(span_live_at(slot), weights, 0.0)
        total = run_total[slot] * factor + jnp.sum(weights.reshape(8, 8, 256), axis=0)
        acc = run_acc[slot] * factor[0:1] + dot_nn(span_vt, weights.astype(BF16))
        for b in FAR:
            if not last:
                later = attend_block(b, queries, later, 1 - side)
            total, acc = collect_block(b, top, total, acc, side)
        total = jnp.sum(total, axis=0, keepdims=True)
        if last:
            run_top[slot] = jnp.broadcast_to(top, (8, 256))
            run_total[slot] = jnp.broadcast_to(total, (8, 256))
            run_acc[slot] = acc
            return None
        publish(slot, top, total, acc)

        @pl.when(slot != 0)
        def _():
            po_copy(slot).start()
            ps_copy(slot).start()

        return jnp.max(later, axis=0, keepdims=True)

    def second_steps(i, top):
        return second_step(2 * i + 1, second_step(2 * i, top, 0), 1)

    queries, top = second_queries(0, 0)
    for b in FAR:
        top = attend_block(b, queries, top, 0)
    top = jnp.max(top, axis=0, keepdims=True)
    top = lax.fori_loop(0, 3, second_steps, top)
    top = second_step(6, top, 0)
    second_step(7, top, 1, last=True)

    def join(one, other):
        top = jnp.maximum(one[0], other[0])
        left = jnp.exp2((one[0] - top) * EXP2_SCALE)
        right = jnp.exp2((other[0] - top) * EXP2_SCALE)
        return top, one[1] * left + other[1] * right, one[2] * left + other[2] * right

    def unpack(stats):
        top = jnp.concatenate([stats[0:1], stats[1:2]], axis=1)
        return top, jnp.concatenate([stats[2:3], stats[3:4]], axis=1)

    def received(slot):
        po_copy(slot).wait_recv()
        ps_copy(slot).wait_recv()
        return unpack(ps_recv[slot]) + (po_recv[slot].astype(F32),)

    sa_forward().wait_recv()
    sp_wide[...] = sp_all[...].reshape(16, 64, HEAD_DIM).astype(F32)
    new_col = iota((32, 128), 1)
    new_owner = select4(new_col // 32, [own_ref[r] for r in range(4)])
    new_row = (s * 4 + c) * 4 + iota((32, 128), 0) % 4
    new_live = (new_owner == new_row) & (new_col % 8 < 4)

    def decode_fresh(k, carry):
        queries = dq_all[pl.ds(2 * k, 2)].reshape(32, HEAD_DIM)
        fresh = (
            sp_wide[:, pl.ds(pl.multiple_of(8 * k, 8), 8), :].reshape(128, HEAD_DIM).astype(BF16)
        )
        stats = dp_send[pl.ds(2 * k, 2), 1].reshape(32, HEAD_DIM)
        former = stats[:, 0:1]
        part = jnp.where(new_live, dot_nt(queries, fresh), NEG)
        top = jnp.maximum(former, jnp.max(part, axis=1, keepdims=True))
        factor = jnp.exp2((former - top) * EXP2_SCALE)
        part = jnp.where(new_live, jnp.exp2((part - top) * EXP2_SCALE), 0.0)
        total = stats[:, 64:65] * factor + jnp.sum(part, axis=1, keepdims=True)
        acc = dp_send[pl.ds(2 * k, 2), 0].reshape(32, HEAD_DIM) * factor
        acc += dot_nn(pltpu.roll(part, 4, axis=1).astype(BF16), fresh)
        dp_send[pl.ds(2 * k, 2), 0] = acc.reshape(2, 16, HEAD_DIM)
        dp_send[pl.ds(2 * k, 2), 1] = jnp.where(left, top, total).reshape(2, 16, HEAD_DIM)
        return carry

    lax.fori_loop(0, 8, decode_fresh, 0)
    for step in range(1, 16):
        dp_copy(step).start()

    publish(4, *join((run_top[4, 0:1, :], run_total[4, 0:1, :], run_acc[4]), received(5)))
    po_copy(4).start()
    ps_copy(4).start()

    state = unpack(ps_send[0]) + (po_send[0].astype(F32),)
    for slot in (1, 6, 7, 2, 3):
        state = join(state, received(slot))

    for step in range(1, 16):
        dp_copy(step).wait_recv()
    dp_recv[0] = dp_send[t]
    tops = [dp_recv[i, 1][:, 0:1] for i in range(16)]
    top = tops[0]
    for i in range(1, 16):
        top = jnp.maximum(top, tops[i])
    acc = jnp.zeros((16, HEAD_DIM), F32)
    total = jnp.zeros((16, 1), F32)
    for i in range(16):
        factor = jnp.exp2((tops[i] - top) * EXP2_SCALE)
        acc += dp_recv[i, 0] * factor
        total += dp_recv[i, 1][:, 64:65] * factor
    d_result[...] = acc / total
    for h in range(4):
        dout_ref[:, h * HEAD_DIM : (h + 1) * HEAD_DIM] = d_result[4 * h : 4 * h + 4, :].astype(BF16)

    _, total, acc = join(state, received(4))
    result = (acc / total).T
    for h in range(4):
        out_ref[0, :, h * HEAD_DIM : (h + 1) * HEAD_DIM] = result[h * 64 : (h + 1) * 64].astype(BF16)

    for step in range(1, 16):
        dq_copy(step).wait_send()
        dp_copy(step).wait_send()
    for step in range(4):
        q_forward(step).wait_send()
    for step in range(1, 4):
        q_copy(step).wait_send()
    for step in range(2):
        for copy in ring_copies(step):
            copy.wait_send()
    sa_forward().wait_send()
    for slot in range(1, 8):
        kv_copy(slot).wait_send()
        sp_copy(slot).wait_send()
        po_copy(slot).wait_send()
        ps_copy(slot).wait_send()


def body(
    span_queries,
    prompt_cache,
    span_kv,
    span_offsets,
    decode_queries,
    decode_cache,
    cache_lengths,
    owner_rows,
):
    vmem = pl.BlockSpec(memory_space=pltpu.VMEM)
    hbm = pl.BlockSpec(memory_space=pltpu.HBM)
    sem = pltpu.SemaphoreType.DMA
    return pl.pallas_call(
        kernel,
        out_shape=(
            pltpu.VMEM(span_queries.shape, BF16),
            pltpu.VMEM(decode_queries.shape, BF16),
        ),
        in_specs=[hbm] * 8,
        out_specs=(vmem, vmem),
        scratch_shapes=[
            pltpu.SMEM((1,), jnp.int32),
            pltpu.SMEM((4,), jnp.int32),
            pltpu.SMEM((4,), jnp.int32),
            pltpu.VMEM((4, 512), BF16),
            pltpu.VMEM((1, 2, 4, 1024), BF16),
            pltpu.VMEM((4, 2, 128, 1024), BF16),
            pltpu.VMEM((8, 2, 256, HEAD_DIM), BF16),
            pltpu.VMEM((8, 2, 256, HEAD_DIM), BF16),
            pltpu.VMEM((HEAD_DIM, 2048), BF16),
            pltpu.VMEM((8, 64, 512), BF16),
            pltpu.VMEM((2, 8, 256, 256), F32),
            pltpu.VMEM((2, 64, 256), F32),
            pltpu.VMEM((8, 8, 256), F32),
            pltpu.VMEM((8, 8, 256), F32),
            pltpu.VMEM((8, HEAD_DIM, 256), F32),
            pltpu.VMEM((8, HEAD_DIM, 256), BF16),
            pltpu.VMEM((8, HEAD_DIM, 256), BF16),
            pltpu.VMEM((8, 8, HEAD_DIM), F32),
            pltpu.VMEM((8, 8, HEAD_DIM), F32),
            pltpu.VMEM((8, 8, HEAD_DIM), F32),
            pltpu.VMEM((8, 8, HEAD_DIM), F32),
            pltpu.VMEM((64, HEAD_DIM), BF16),
            pltpu.VMEM((2, 2, 4, 64, HEAD_DIM), BF16),
            pltpu.VMEM((16, 64, HEAD_DIM), F32),
            pltpu.VMEM((16, HEAD_DIM), F32),
            pltpu.VMEM((16, HEAD_DIM), BF16),
            pltpu.VMEM((16, 16, HEAD_DIM), BF16),
            pltpu.VMEM((16, 2, 16, HEAD_DIM), F32),
            pltpu.VMEM((16, 2, 16, HEAD_DIM), F32),
            pltpu.VMEM((16, HEAD_DIM), F32),
            sem((8,)),
            sem((8,)),
            sem((8,)),
            sem((8,)),
            sem((8,)),
            sem((8,)),
            sem((8,)),
            sem((8,)),
            sem(()),
            sem(()),
            sem((8,)),
            sem((8,)),
            sem((16,)),
            sem((16,)),
            sem((16,)),
            sem((16,)),
            sem((8,)),
            sem((8,)),
            sem((8,)),
            sem((8,)),
        ],
        compiler_params=pltpu.CompilerParams(
            collective_id=0, has_side_effects=True, vmem_limit_bytes=60 * 1024 * 1024
        ),
    )(
        span_offsets,
        cache_lengths,
        owner_rows,
        decode_queries,
        span_kv,
        span_queries,
        prompt_cache,
        decode_cache,
    )


def solution(mesh):
    return jax.shard_map(
        body,
        mesh=mesh,
        in_specs=(
            P("sect", "ctx", "tp"),
            P("sect", None, ("ctx", "tp"), None),
            P("sect", None, ("ctx", "tp"), None),
            P("sect"),
            P(("sect", "ctx"), "tp"),
            P(("sect", "ctx"), None, "tp", None),
            P(("sect", "ctx")),
            P(),
        ),
        out_specs=(P("sect", "ctx", "tp"), P(("sect", "ctx"), "tp")),
        check_vma=False,
    )
```

```python
import math

import jax
import jax.numpy as jnp
from jax import lax
from jax.experimental import pallas as pl
from jax.experimental.pallas import tpu as pltpu
from jax.sharding import PartitionSpec as P

HEAD_DIM = 128
MESH = pl.DeviceIdType.MESH
NEG = -1e30
EXP2_SCALE = math.log2(math.e) / math.sqrt(HEAD_DIM)
F32 = jnp.float32
BF16 = jnp.bfloat16
NEAR = (0, 1, 2, 6, 3, 7)
FAR = (4, 5)


def dot_nt(a, b):
    return lax.dot_general(a, b, (((1,), (1,)), ((), ())), preferred_element_type=F32)


def dot_nn(a, b):
    return lax.dot_general(a, b, (((1,), (0,)), ((), ())), preferred_element_type=F32)


def iota(shape, dim):
    return lax.broadcasted_iota(jnp.int32, shape, dim)


def select4(index, values):
    return jnp.where(
        index == 0,
        values[0],
        jnp.where(index == 1, values[1], jnp.where(index == 2, values[2], values[3])),
    )


def kernel(
    off_hbm,
    len_hbm,
    own_hbm,
    dq_hbm,
    skv_hbm,
    q_hbm,
    pc_hbm,
    dc_hbm,
    out_ref,
    dout_ref,
    off_ref,
    len_ref,
    own_ref,
    dq_ref,
    skv_ref,
    cache,
    staged,
    kv,
    vt,
    q_all,
    scores,
    span_scores,
    run_top,
    run_total,
    run_acc,
    po_send,
    po_recv,
    ps_send,
    ps_recv,
    sp_head,
    sp_pre,
    sp_block,
    sp_all,
    sp_wide,
    dq_wide,
    dq_block,
    dq_all,
    dp_send,
    dp_out,
    dp_recv,
    d_result,
    local_sem,
    stage_sem,
    kv_ssem,
    kv_rsem,
    q_ssem,
    q_rsem,
    sp_ssem,
    sp_rsem,
    sa_ssem,
    sa_rsem,
    ring_ssem,
    ring_rsem,
    dq_ssem,
    dq_rsem,
    dp_ssem,
    dp_rsem,
    po_ssem,
    po_rsem,
    ps_ssem,
    ps_rsem,
):
    s = lax.axis_index("sect")
    c = lax.axis_index("ctx")
    t = lax.axis_index("tp")
    y = t // 4
    x = t % 4
    head = t // 2
    pair = t + 1 - 2 * (t % 2)

    def kv_peer(slot, sign):
        a, b = slot // 2, slot % 2
        far_y = (y + sign * a + 4) % 4
        far_x = x + b * (3 - 2 * x)
        return far_y * 4 + far_x

    def q_peer(slot, sign):
        a, b = slot // 2, slot % 2
        return (c + sign * a + 4) % 4, t + b * (pair - t)

    core = s % 2
    layer = (s // 2) * 4 + c

    def kv_copy(slot):
        far = kv_peer(slot, 1)
        return pltpu.make_async_remote_copy(
            src_ref=staged.at[far // 2],
            dst_ref=kv.at[slot],
            send_sem=kv_ssem.at[slot],
            recv_sem=kv_rsem.at[slot],
            device_id=(s, c, far),
            device_id_type=MESH,
        )

    def q_copy(step):
        return pltpu.make_async_remote_copy(
            src_ref=q_all.at[0],
            dst_ref=q_all.at[2 * step],
            send_sem=q_ssem.at[2 * step],
            recv_sem=q_rsem.at[2 * step],
            device_id=(s, (c + step) % 4, t),
            device_id_type=MESH,
        )

    def q_forward(step):
        return pltpu.make_async_remote_copy(
            src_ref=q_all.at[2 * step],
            dst_ref=q_all.at[2 * step + 1],
            send_sem=q_ssem.at[2 * step + 1],
            recv_sem=q_rsem.at[2 * step + 1],
            device_id=(s, c, pair),
            device_id_type=MESH,
        )

    def sp_copy(slot):
        far = kv_peer(slot, 1)
        return pltpu.make_async_remote_copy(
            src_ref=sp_head.at[far // 2],
            dst_ref=sp_pre.at[slot],
            send_sem=sp_ssem.at[slot],
            recv_sem=sp_rsem.at[slot],
            device_id=(s, c, far),
            device_id_type=MESH,
        )

    def ring_peer(shift):
        far = (layer + shift + 8) % 8
        return (far // 4) * 2 + core, far % 4

    ring_steps = (((0, 1), (0, -1), (0, 2), (0, -2)), ((1, -2), (2, -2), (-1, 2)))

    def ring_copies(step):
        for index, (block, shift) in enumerate(ring_steps[step]):
            far_s, far_c = ring_peer(shift)
            moved = (layer + block + 8) % 8
            yield pltpu.make_async_remote_copy(
                src_ref=sp_all.at[moved // 4, core, moved % 4],
                dst_ref=sp_all.at[moved // 4, core, moved % 4],
                send_sem=ring_ssem.at[4 * step + index],
                recv_sem=ring_rsem.at[4 * step + index],
                device_id=(far_s, far_c, t),
                device_id_type=MESH,
            )

    def ring_start(step):
        for copy in ring_copies(step):
            copy.start()

    def ring_wait(step):
        for copy in ring_copies(step):
            copy.wait_recv()

    def sa_forward():
        return pltpu.make_async_remote_copy(
            src_ref=sp_all.at[:, core],
            dst_ref=sp_all.at[:, core],
            send_sem=sa_ssem,
            recv_sem=sa_rsem,
            device_id=(s + 1 - 2 * core, c, t),
            device_id_type=MESH,
        )

    def dq_copy(step):
        return pltpu.make_async_remote_copy(
            src_ref=dq_block,
            dst_ref=dq_all.at[t],
            send_sem=dq_ssem.at[step],
            recv_sem=dq_rsem.at[step],
            device_id=(s, c, (t + step) % 16),
            device_id_type=MESH,
        )

    def dp_copy(step):
        far = (t + step) % 16
        return pltpu.make_async_remote_copy(
            src_ref=dp_out.at[far],
            dst_ref=dp_recv.at[step],
            send_sem=dp_ssem.at[step],
            recv_sem=dp_rsem.at[step],
            device_id=(s, c, far),
            device_id_type=MESH,
        )

    def sum_peer(slot):
        far_c, far_t = q_peer(slot, -1)
        return jnp.where(slot == 5, c, far_c), far_t

    def po_copy(slot):
        far_c, far_t = sum_peer(slot)
        return pltpu.make_async_remote_copy(
            src_ref=po_send.at[slot],
            dst_ref=po_recv.at[slot],
            send_sem=po_ssem.at[slot],
            recv_sem=po_rsem.at[slot],
            device_id=(s, far_c, far_t),
            device_id_type=MESH,
        )

    def ps_copy(slot):
        far_c, far_t = sum_peer(slot)
        return pltpu.make_async_remote_copy(
            src_ref=ps_send.at[slot],
            dst_ref=ps_recv.at[slot],
            send_sem=ps_ssem.at[slot],
            recv_sem=ps_rsem.at[slot],
            device_id=(s, far_c, far_t),
            device_id_type=MESH,
        )

    barrier = pltpu.get_barrier_semaphore()

    def greet(far_s, far_c, far_t):
        pl.semaphore_signal(
            barrier, inc=1, device_id=(far_s, far_c, far_t), device_id_type=MESH
        )

    for shift in (2, -2, 1, -1):
        far_s, far_c = ring_peer(shift)
        greet(far_s, far_c, t)
    for step in range(1, 16):
        greet(s, c, (t + step) % 16)
    for step in range(1, 4):
        greet(s, (c + step) % 4, t)
        greet(s, (c + step) % 4, pair)
    greet(s + 1 - 2 * core, c, t)

    own_column = pl.multiple_of(head * HEAD_DIM, HEAD_DIM)
    local_small = [
        pltpu.make_async_copy(source, target, local_sem.at[3 + i])
        for i, (source, target) in enumerate(
            [
                (dq_hbm, dq_ref),
                (skv_hbm, skv_ref),
                (off_hbm, off_ref),
                (len_hbm, len_ref),
                (own_hbm, own_ref),
            ]
        )
    ]
    for copy in local_small:
        copy.start()
    local_kv = pltpu.make_async_copy(
        pc_hbm.at[0, :, :, pl.ds(own_column, HEAD_DIM)], kv.at[0], local_sem.at[0]
    )
    local_q = pltpu.make_async_copy(q_hbm.at[0], q_all.at[0], local_sem.at[1])
    local_cache = pltpu.make_async_copy(dc_hbm, cache, local_sem.at[2])
    local_q.start()
    stage = [
        pltpu.make_async_copy(
            pc_hbm.at[0, :, :, h * HEAD_DIM : (h + 1) * HEAD_DIM], staged.at[h], stage_sem.at[h]
        )
        for h in range(8)
    ]
    for copy in stage:
        copy.start()
    local_kv.start()
    local_cache.start()

    for copy in local_small:
        copy.wait()
    own_q = dq_ref[...].astype(F32)
    span_k = skv_ref[0, 0].astype(F32)
    span_v = skv_ref[0, 1].astype(F32)
    for h in range(4):
        dq_wide[4 * h : 4 * h + 4, :] = own_q[:, h * HEAD_DIM : (h + 1) * HEAD_DIM]
    for h in range(8):
        sp_head[h, 0:4, :] = span_k[:, h * HEAD_DIM : (h + 1) * HEAD_DIM]
        sp_head[h, 4:8, :] = span_v[:, h * HEAD_DIM : (h + 1) * HEAD_DIM]
    dq_block[...] = dq_wide[...].astype(BF16)
    sp_block[...] = sp_head[...].reshape(64, HEAD_DIM).astype(BF16)
    dq_all[t] = dq_block[...]
    sp_all[s // 2, core, c] = sp_block[...]
    sp_pre[0] = sp_head[head]
    local_q.wait()
    for copy in stage:
        copy.wait()

    pl.semaphore_wait(barrier, 26)

    for step in range(1, 16):
        dq_copy(step).start()
    ring_start(0)
    for slot in NEAR[1:]:
        kv_copy(slot).start()
    q_forward(0).start()
    for step in range(1, 4):
        q_copy(step).start()
    for slot in FAR:
        kv_copy(slot).start()
    for slot in range(1, 8):
        sp_copy(slot).start()

    local_cache.wait()
    for step in range(1, 16):
        dq_copy(step).wait_recv()
    row_q = iota((32, 512), 0) % 4
    row_p = iota((32, 512), 1) // 128
    pos = t * 128 + iota((32, 512), 1) % 128
    length = select4(row_p, [len_ref[r] for r in range(4)])
    cache_live = (row_q == row_p) & (pos < length)
    left = iota((32, 128), 1) < 64

    def decode_cached(k, carry):
        column = pl.ds(pl.multiple_of(k * HEAD_DIM, HEAD_DIM), HEAD_DIM)
        queries = dq_all[pl.ds(2 * k, 2)].reshape(32, HEAD_DIM)
        part = jnp.concatenate(
            [dot_nt(queries, cache[r, 0, :, column]) for r in range(4)], axis=1
        )
        part = jnp.where(cache_live, part, NEG)
        top = jnp.max(part, axis=1, keepdims=True)
        part = jnp.exp2((part - top) * EXP2_SCALE)
        total = jnp.sum(part, axis=1, keepdims=True)
        rounded = part.astype(BF16)
        acc = jnp.zeros((32, HEAD_DIM), F32)
        for r in range(4):
            acc += dot_nn(rounded[:, r * 128 : (r + 1) * 128], cache[r, 1, :, column])
        dp_send[pl.ds(2 * k, 2), 0] = acc.reshape(2, 16, HEAD_DIM)
        dp_send[pl.ds(2 * k, 2), 1] = jnp.where(left, top, total).reshape(2, 16, HEAD_DIM)
        return carry

    lax.fori_loop(0, 4, decode_cached, 0, unroll=True)
    for step in (1, 3):
        q_copy(step).wait_recv()
        q_forward(step).start()
    lax.fori_loop(4, 8, decode_cached, 0, unroll=True)
    q_copy(2).wait_recv()
    q_forward(2).start()
    ring_wait(0)
    ring_start(1)

    local_kv.wait()
    offset = off_ref[0]

    def load_queries(slot):
        block = q_all[slot]
        return jnp.concatenate(
            [block[:, h * HEAD_DIM : (h + 1) * HEAD_DIM] for h in range(4)], axis=0
        )

    def attend_block(b, queries, top, side):
        start = (c * 16 + kv_peer(b, -1)) * 256
        part = dot_nt(kv[b, 0], queries)
        part = jnp.where(start + iota((256, 256), 0) < offset, part, NEG)
        scores[side, b] = part
        return jnp.maximum(top, jnp.max(part.reshape(32, 8, 256), axis=0))

    def collect_block(b, top, total, acc, side):
        weights = jnp.exp2((scores[side, b] - top) * EXP2_SCALE)
        total += jnp.sum(weights.reshape(32, 8, 256), axis=0)
        acc += dot_nn(vt[:, b * 256 : (b + 1) * 256], weights.astype(BF16))
        return total, acc

    def transpose_values(slots):
        for slot in slots:
            vt[:, slot * 256 : (slot + 1) * 256] = kv[slot, 1].astype(F32).T.astype(BF16)

    for slot in NEAR[1:]:
        kv_copy(slot).wait_recv()
    transpose_values(NEAR)

    def first_queries(i):
        slot = (2 * i) % 8 + i // 4

        @pl.when(slot % 2 == 1)
        def _():
            q_forward(slot // 2).wait_recv()

        return load_queries(slot)

    def first_step(i, top, side, last=False):
        slot = (2 * i) % 8 + i // 4
        queries = None if last else first_queries(i + 1)
        total, acc = jnp.zeros((8, 256), F32), jnp.zeros((HEAD_DIM, 256), F32)
        later = jnp.full((8, 256), NEG, F32)
        for b in NEAR:
            if not last:
                later = attend_block(b, queries, later, 1 - side)
            total, acc = collect_block(b, top, total, acc, side)
        run_top[slot] = jnp.broadcast_to(top, (8, 256))
        run_total[slot] = total
        run_acc[slot] = acc
        return jnp.max(later, axis=0, keepdims=True)

    def first_steps(i, top):
        return first_step(2 * i + 1, first_step(2 * i, top, 0), 1)

    top = jnp.full((8, 256), NEG, F32)
    queries = load_queries(0)
    for b in NEAR:
        top = attend_block(b, queries, top, 0)
    top = jnp.max(top, axis=0, keepdims=True)
    top = lax.fori_loop(0, 2, first_steps, top)
    ring_wait(1)
    sa_forward().start()
    top = lax.fori_loop(2, 3, first_steps, top)
    top = first_step(6, top, 0)
    first_step(7, top, 1, last=True)

    for slot in range(1, 8):
        sp_copy(slot).wait_recv()
    for slot in FAR:
        kv_copy(slot).wait_recv()
    transpose_values(FAR)
    span_rows = sp_pre[...].reshape(64, HEAD_DIM)
    span_keys = span_rows.astype(BF16)
    span_vt = pltpu.roll(span_rows, 60, axis=0).T.astype(BF16)
    span_row = iota((64, 256), 0)
    span_slot = span_row // 8
    span_y = (y - span_slot // 2 + 4) % 4
    span_x = x + (span_slot % 2) * (3 - 2 * x)
    span_token = (c * 16 + span_y * 4 + span_x) * 4 + span_row % 8
    span_real = span_row % 8 < 4

    def publish(slot, top, total, acc):
        po_send[slot] = acc.astype(BF16)
        row = iota((8, HEAD_DIM), 0)
        tops = jnp.where(row % 2 == 0, top[:, :HEAD_DIM], top[:, HEAD_DIM:])
        totals = jnp.where(row % 2 == 0, total[:, :HEAD_DIM], total[:, HEAD_DIM:])
        ps_send[slot] = jnp.where(row < 2, tops, totals)

    def span_live_at(slot):
        far_c, _ = q_peer(slot, -1)
        return span_real & (span_token <= far_c * 64 + iota((64, 256), 1) % 64)

    def second_queries(i, side):
        slot = (i + 5) % 8
        queries = load_queries(slot)
        part = jnp.where(span_live_at(slot), dot_nt(span_keys, queries), NEG)
        span_scores[side] = part
        top = jnp.maximum(run_top[slot], jnp.max(part.reshape(8, 8, 256), axis=0))
        return queries, top

    def second_step(i, top, side, last=False):
        slot = (i + 5) % 8
        queries, later = (None, None) if last else second_queries(i + 1, 1 - side)
        factor = jnp.exp2((run_top[slot] - top) * EXP2_SCALE)
        weights = jnp.exp2((span_scores[side] - top) * EXP2_SCALE)
        weights = jnp.where(span_live_at(slot), weights, 0.0)
        total = run_total[slot] * factor + jnp.sum(weights.reshape(8, 8, 256), axis=0)
        acc = run_acc[slot] * factor[0:1] + dot_nn(span_vt, weights.astype(BF16))
        for b in FAR:
            if not last:
                later = attend_block(b, queries, later, 1 - side)
            total, acc = collect_block(b, top, total, acc, side)
        total = jnp.sum(total, axis=0, keepdims=True)
        if last:
            run_top[slot] = jnp.broadcast_to(top, (8, 256))
            run_total[slot] = jnp.broadcast_to(total, (8, 256))
            run_acc[slot] = acc
            return None
        publish(slot, top, total, acc)

        @pl.when(slot != 0)
        def _():
            po_copy(slot).start()
            ps_copy(slot).start()

        return jnp.max(later, axis=0, keepdims=True)

    def second_steps(i, top):
        return second_step(2 * i + 1, second_step(2 * i, top, 0), 1)

    queries, top = second_queries(0, 0)
    for b in FAR:
        top = attend_block(b, queries, top, 0)
    top = jnp.max(top, axis=0, keepdims=True)
    top = lax.fori_loop(0, 3, second_steps, top)
    top = second_step(6, top, 0)
    second_step(7, top, 1, last=True)

    def join(one, other):
        top = jnp.maximum(one[0], other[0])
        left = jnp.exp2((one[0] - top) * EXP2_SCALE)
        right = jnp.exp2((other[0] - top) * EXP2_SCALE)
        return top, one[1] * left + other[1] * right, one[2] * left + other[2] * right

    def unpack(stats):
        top = jnp.concatenate([stats[0:1], stats[1:2]], axis=1)
        return top, jnp.concatenate([stats[2:3], stats[3:4]], axis=1)

    def received(slot):
        po_copy(slot).wait_recv()
        ps_copy(slot).wait_recv()
        return unpack(ps_recv[slot]) + (po_recv[slot].astype(F32),)

    sa_forward().wait_recv()
    sp_wide[...] = sp_all[...].reshape(16, 64, HEAD_DIM).astype(F32)
    new_col = iota((32, 128), 1)
    new_owner = select4(new_col // 32, [own_ref[r] for r in range(4)])
    new_row = (s * 4 + c) * 4 + iota((32, 128), 0) % 4
    new_live = (new_owner == new_row) & (new_col % 8 < 4)

    def decode_fresh(k, carry):
        queries = dq_all[pl.ds(2 * k, 2)].reshape(32, HEAD_DIM)
        fresh = (
            sp_wide[:, pl.ds(pl.multiple_of(8 * k, 8), 8), :].reshape(128, HEAD_DIM).astype(BF16)
        )
        stats = dp_send[pl.ds(2 * k, 2), 1].reshape(32, HEAD_DIM)
        former = stats[:, 0:1]
        part = jnp.where(new_live, dot_nt(queries, fresh), NEG)
        top = jnp.maximum(former, jnp.max(part, axis=1, keepdims=True))
        factor = jnp.exp2((former - top) * EXP2_SCALE)
        part = jnp.where(new_live, jnp.exp2((part - top) * EXP2_SCALE), 0.0)
        total = stats[:, 64:65] * factor + jnp.sum(part, axis=1, keepdims=True)
        acc = dp_send[pl.ds(2 * k, 2), 0].reshape(32, HEAD_DIM) * factor
        acc += dot_nn(pltpu.roll(part, 4, axis=1).astype(BF16), fresh)
        dp_out[pl.ds(2 * k, 2), 0] = acc.astype(BF16).reshape(2, 16, HEAD_DIM)
        pieces = jnp.zeros((32, HEAD_DIM), F32)
        lane = iota((32, HEAD_DIM), 1) // 16
        for first, value in ((0, top), (3, total)):
            for index in range(first, first + 3):
                piece = value.astype(BF16).astype(F32)
                pieces = jnp.where(lane == index, piece, pieces)
                value = value - piece
        dp_out[pl.ds(2 * k, 2), 1] = pieces.astype(BF16).reshape(2, 16, HEAD_DIM)
        return carry

    lax.fori_loop(0, 8, decode_fresh, 0, unroll=True)
    for step in range(1, 16):
        dp_copy(step).start()

    publish(4, *join((run_top[4, 0:1, :], run_total[4, 0:1, :], run_acc[4]), received(5)))
    po_copy(4).start()
    ps_copy(4).start()

    state = unpack(ps_send[0]) + (po_send[0].astype(F32),)
    for slot in (1, 6, 7, 2, 3):
        state = join(state, received(slot))

    for step in range(1, 16):
        dp_copy(step).wait_recv()
    dp_recv[0] = dp_out[t]
    stats = [dp_recv[i, 1].astype(F32) for i in range(16)]
    tops = [v[:, 0:1] + v[:, 16:17] + v[:, 32:33] for v in stats]
    totals = [v[:, 48:49] + v[:, 64:65] + v[:, 80:81] for v in stats]
    top = tops[0]
    for i in range(1, 16):
        top = jnp.maximum(top, tops[i])
    acc = jnp.zeros((16, HEAD_DIM), F32)
    total = jnp.zeros((16, 1), F32)
    for i in range(16):
        factor = jnp.exp2((tops[i] - top) * EXP2_SCALE)
        acc += dp_recv[i, 0].astype(F32) * factor
        total += totals[i] * factor
    d_result[...] = acc / total
    for h in range(4):
        dout_ref[:, h * HEAD_DIM : (h + 1) * HEAD_DIM] = d_result[4 * h : 4 * h + 4, :].astype(BF16)

    _, total, acc = join(state, received(4))
    result = (acc / total).T
    for h in range(4):
        out_ref[0, :, h * HEAD_DIM : (h + 1) * HEAD_DIM] = result[h * 64 : (h + 1) * 64].astype(BF16)

    for step in range(1, 16):
        dq_copy(step).wait_send()
        dp_copy(step).wait_send()
    for step in range(4):
        q_forward(step).wait_send()
    for step in range(1, 4):
        q_copy(step).wait_send()
    for step in range(2):
        for copy in ring_copies(step):
            copy.wait_send()
    sa_forward().wait_send()
    for slot in range(1, 8):
        kv_copy(slot).wait_send()
        sp_copy(slot).wait_send()
        po_copy(slot).wait_send()
        ps_copy(slot).wait_send()


def body(
    span_queries,
    prompt_cache,
    span_kv,
    span_offsets,
    decode_queries,
    decode_cache,
    cache_lengths,
    owner_rows,
):
    vmem = pl.BlockSpec(memory_space=pltpu.VMEM)
    hbm = pl.BlockSpec(memory_space=pltpu.HBM)
    sem = pltpu.SemaphoreType.DMA
    return pl.pallas_call(
        kernel,
        out_shape=(
            pltpu.VMEM(span_queries.shape, BF16),
            pltpu.VMEM(decode_queries.shape, BF16),
        ),
        in_specs=[hbm] * 8,
        out_specs=(vmem, vmem),
        scratch_shapes=[
            pltpu.SMEM((1,), jnp.int32),
            pltpu.SMEM((4,), jnp.int32),
            pltpu.SMEM((4,), jnp.int32),
            pltpu.VMEM((4, 512), BF16),
            pltpu.VMEM((1, 2, 4, 1024), BF16),
            pltpu.VMEM((4, 2, 128, 1024), BF16),
            pltpu.VMEM((8, 2, 256, HEAD_DIM), BF16),
            pltpu.VMEM((8, 2, 256, HEAD_DIM), BF16),
            pltpu.VMEM((HEAD_DIM, 2048), BF16),
            pltpu.VMEM((8, 64, 512), BF16),
            pltpu.VMEM((2, 8, 256, 256), F32),
            pltpu.VMEM((2, 64, 256), F32),
            pltpu.VMEM((8, 8, 256), F32),
            pltpu.VMEM((8, 8, 256), F32),
            pltpu.VMEM((8, HEAD_DIM, 256), F32),
            pltpu.VMEM((8, HEAD_DIM, 256), BF16),
            pltpu.VMEM((8, HEAD_DIM, 256), BF16),
            pltpu.VMEM((8, 8, HEAD_DIM), F32),
            pltpu.VMEM((8, 8, HEAD_DIM), F32),
            pltpu.VMEM((8, 8, HEAD_DIM), F32),
            pltpu.VMEM((8, 8, HEAD_DIM), F32),
            pltpu.VMEM((64, HEAD_DIM), BF16),
            pltpu.VMEM((2, 2, 4, 64, HEAD_DIM), BF16),
            pltpu.VMEM((16, 64, HEAD_DIM), F32),
            pltpu.VMEM((16, HEAD_DIM), F32),
            pltpu.VMEM((16, HEAD_DIM), BF16),
            pltpu.VMEM((16, 16, HEAD_DIM), BF16),
            pltpu.VMEM((16, 2, 16, HEAD_DIM), F32),
            pltpu.VMEM((16, 2, 16, HEAD_DIM), BF16),
            pltpu.VMEM((16, 2, 16, HEAD_DIM), BF16),
            pltpu.VMEM((16, HEAD_DIM), F32),
            sem((8,)),
            sem((8,)),
            sem((8,)),
            sem((8,)),
            sem((8,)),
            sem((8,)),
            sem((8,)),
            sem((8,)),
            sem(()),
            sem(()),
            sem((8,)),
            sem((8,)),
            sem((16,)),
            sem((16,)),
            sem((16,)),
            sem((16,)),
            sem((8,)),
            sem((8,)),
            sem((8,)),
            sem((8,)),
        ],
        compiler_params=pltpu.CompilerParams(
            collective_id=0, has_side_effects=True, vmem_limit_bytes=60 * 1024 * 1024
        ),
    )(
        span_offsets,
        cache_lengths,
        owner_rows,
        decode_queries,
        span_kv,
        span_queries,
        prompt_cache,
        decode_cache,
    )


def solution(mesh):
    return jax.shard_map(
        body,
        mesh=mesh,
        in_specs=(
            P("sect", "ctx", "tp"),
            P("sect", None, ("ctx", "tp"), None),
            P("sect", None, ("ctx", "tp"), None),
            P("sect"),
            P(("sect", "ctx"), "tp"),
            P(("sect", "ctx"), None, "tp", None),
            P(("sect", "ctx")),
            P(),
        ),
        out_specs=(P("sect", "ctx", "tp"), P(("sect", "ctx"), "tp")),
        check_vma=False,
    )
```

```python
import math

import jax
import jax.numpy as jnp
from jax import lax
from jax.experimental import pallas as pl
from jax.experimental.pallas import tpu as pltpu
from jax.sharding import PartitionSpec as P

HEAD_DIM = 128
MESH = pl.DeviceIdType.MESH
NEG = -1e30
EXP2_SCALE = math.log2(math.e) / math.sqrt(HEAD_DIM)
F32 = jnp.float32
BF16 = jnp.bfloat16
NEAR = (0, 1, 2, 6, 3, 7)
FAR = (4, 5)
FAR_FIRST = (10, 9, 11, 6, 14, 8, 2, 5, 7, 13, 15, 1, 3, 4, 12)


def dot_nt(a, b):
    return lax.dot_general(a, b, (((1,), (1,)), ((), ())), preferred_element_type=F32)


def dot_nn(a, b):
    return lax.dot_general(a, b, (((1,), (0,)), ((), ())), preferred_element_type=F32)


def iota(shape, dim):
    return lax.broadcasted_iota(jnp.int32, shape, dim)


def select4(index, values):
    return jnp.where(
        index == 0,
        values[0],
        jnp.where(index == 1, values[1], jnp.where(index == 2, values[2], values[3])),
    )


def kernel(
    off_hbm,
    len_hbm,
    own_hbm,
    dq_hbm,
    skv_hbm,
    q_hbm,
    pc_hbm,
    dc_hbm,
    out_ref,
    dout_ref,
    off_ref,
    len_ref,
    own_ref,
    dq_ref,
    skv_ref,
    cache,
    staged,
    kv,
    vt,
    q_all,
    scores,
    span_scores,
    run_top,
    run_total,
    run_acc,
    po_send,
    po_recv,
    ps_send,
    ps_recv,
    sp_head,
    sp_pre,
    sp_block,
    sp_all,
    sp_wide,
    dq_wide,
    dq_block,
    dq_all,
    dp_send,
    dp_out,
    dp_recv,
    d_result,
    local_sem,
    stage_sem,
    kv_ssem,
    kv_rsem,
    q_ssem,
    q_rsem,
    sp_ssem,
    sp_rsem,
    sa_ssem,
    sa_rsem,
    ring_ssem,
    ring_rsem,
    dq_ssem,
    dq_rsem,
    dp_ssem,
    dp_rsem,
    po_ssem,
    po_rsem,
    ps_ssem,
    ps_rsem,
):
    s = lax.axis_index("sect")
    c = lax.axis_index("ctx")
    t = lax.axis_index("tp")
    y = t // 4
    x = t % 4
    head = t // 2
    pair = t + 1 - 2 * (t % 2)

    def kv_peer(slot, sign):
        a, b = slot // 2, slot % 2
        far_y = (y + sign * a + 4) % 4
        far_x = x + b * (3 - 2 * x)
        return far_y * 4 + far_x

    def q_peer(slot, sign):
        a, b = slot // 2, slot % 2
        return (c + sign * a + 4) % 4, t + b * (pair - t)

    core = s % 2
    layer = (s // 2) * 4 + c

    def kv_copy(slot):
        far = kv_peer(slot, 1)
        return pltpu.make_async_remote_copy(
            src_ref=staged.at[far // 2],
            dst_ref=kv.at[slot],
            send_sem=kv_ssem.at[slot],
            recv_sem=kv_rsem.at[slot],
            device_id=(s, c, far),
            device_id_type=MESH,
        )

    def q_copy(step):
        return pltpu.make_async_remote_copy(
            src_ref=q_all.at[0],
            dst_ref=q_all.at[2 * step],
            send_sem=q_ssem.at[2 * step],
            recv_sem=q_rsem.at[2 * step],
            device_id=(s, (c + step) % 4, t),
            device_id_type=MESH,
        )

    def q_forward(step):
        return pltpu.make_async_remote_copy(
            src_ref=q_all.at[2 * step],
            dst_ref=q_all.at[2 * step + 1],
            send_sem=q_ssem.at[2 * step + 1],
            recv_sem=q_rsem.at[2 * step + 1],
            device_id=(s, c, pair),
            device_id_type=MESH,
        )

    def sp_copy(slot):
        far = kv_peer(slot, 1)
        return pltpu.make_async_remote_copy(
            src_ref=sp_head.at[far // 2],
            dst_ref=sp_pre.at[slot],
            send_sem=sp_ssem.at[slot],
            recv_sem=sp_rsem.at[slot],
            device_id=(s, c, far),
            device_id_type=MESH,
        )

    def ring_peer(shift):
        far = (layer + shift + 8) % 8
        return (far // 4) * 2 + core, far % 4

    ring_steps = (((0, 1), (0, -1), (0, 2), (0, -2)), ((1, -2), (2, -2), (-1, 2)))

    def ring_copies(step):
        for index, (block, shift) in enumerate(ring_steps[step]):
            far_s, far_c = ring_peer(shift)
            moved = (layer + block + 8) % 8
            yield pltpu.make_async_remote_copy(
                src_ref=sp_all.at[moved // 4, core, moved % 4],
                dst_ref=sp_all.at[moved // 4, core, moved % 4],
                send_sem=ring_ssem.at[4 * step + index],
                recv_sem=ring_rsem.at[4 * step + index],
                device_id=(far_s, far_c, t),
                device_id_type=MESH,
            )

    def ring_start(step):
        for copy in ring_copies(step):
            copy.start()

    def ring_wait(step):
        for copy in ring_copies(step):
            copy.wait_recv()

    def sa_forward():
        return pltpu.make_async_remote_copy(
            src_ref=sp_all.at[:, core],
            dst_ref=sp_all.at[:, core],
            send_sem=sa_ssem,
            recv_sem=sa_rsem,
            device_id=(s + 1 - 2 * core, c, t),
            device_id_type=MESH,
        )

    def dq_copy(step):
        return pltpu.make_async_remote_copy(
            src_ref=dq_block,
            dst_ref=dq_all.at[t],
            send_sem=dq_ssem.at[step],
            recv_sem=dq_rsem.at[step],
            device_id=(s, c, (t + step) % 16),
            device_id_type=MESH,
        )

    def dp_copy(step):
        far = (t + step) % 16
        return pltpu.make_async_remote_copy(
            src_ref=dp_out.at[far],
            dst_ref=dp_recv.at[step],
            send_sem=dp_ssem.at[step],
            recv_sem=dp_rsem.at[step],
            device_id=(s, c, far),
            device_id_type=MESH,
        )

    def sum_peer(slot):
        far_c, far_t = q_peer(slot, -1)
        return jnp.where(slot == 5, c, far_c), far_t

    def po_copy(slot):
        far_c, far_t = sum_peer(slot)
        return pltpu.make_async_remote_copy(
            src_ref=po_send.at[slot],
            dst_ref=po_recv.at[slot],
            send_sem=po_ssem.at[slot],
            recv_sem=po_rsem.at[slot],
            device_id=(s, far_c, far_t),
            device_id_type=MESH,
        )

    def ps_copy(slot):
        far_c, far_t = sum_peer(slot)
        return pltpu.make_async_remote_copy(
            src_ref=ps_send.at[slot],
            dst_ref=ps_recv.at[slot],
            send_sem=ps_ssem.at[slot],
            recv_sem=ps_rsem.at[slot],
            device_id=(s, far_c, far_t),
            device_id_type=MESH,
        )

    barrier = pltpu.get_barrier_semaphore()

    def greet(far_s, far_c, far_t):
        pl.semaphore_signal(
            barrier, inc=1, device_id=(far_s, far_c, far_t), device_id_type=MESH
        )

    for shift in (2, -2, 1, -1):
        far_s, far_c = ring_peer(shift)
        greet(far_s, far_c, t)
    for step in range(1, 16):
        greet(s, c, (t + step) % 16)
    for step in range(1, 4):
        greet(s, (c + step) % 4, t)
        greet(s, (c + step) % 4, pair)
    greet(s + 1 - 2 * core, c, t)

    own_column = pl.multiple_of(head * HEAD_DIM, HEAD_DIM)
    local_small = [
        pltpu.make_async_copy(source, target, local_sem.at[3 + i])
        for i, (source, target) in enumerate(
            [
                (dq_hbm, dq_ref),
                (skv_hbm, skv_ref),
                (off_hbm, off_ref),
                (len_hbm, len_ref),
                (own_hbm, own_ref),
            ]
        )
    ]
    for copy in local_small:
        copy.start()
    local_kv = pltpu.make_async_copy(
        pc_hbm.at[0, :, :, pl.ds(own_column, HEAD_DIM)], kv.at[0], local_sem.at[0]
    )
    local_q = pltpu.make_async_copy(q_hbm.at[0], q_all.at[0], local_sem.at[1])
    local_cache = pltpu.make_async_copy(dc_hbm, cache, local_sem.at[2])
    local_q.start()
    stage = [
        pltpu.make_async_copy(
            pc_hbm.at[0, :, :, h * HEAD_DIM : (h + 1) * HEAD_DIM], staged.at[h], stage_sem.at[h]
        )
        for h in range(8)
    ]
    for copy in stage:
        copy.start()
    local_kv.start()
    local_cache.start()

    for copy in local_small:
        copy.wait()
    own_q = dq_ref[...].astype(F32)
    span_k = skv_ref[0, 0].astype(F32)
    span_v = skv_ref[0, 1].astype(F32)
    for h in range(4):
        dq_wide[4 * h : 4 * h + 4, :] = own_q[:, h * HEAD_DIM : (h + 1) * HEAD_DIM]
    for h in range(8):
        sp_head[h, 0:4, :] = span_k[:, h * HEAD_DIM : (h + 1) * HEAD_DIM]
        sp_head[h, 4:8, :] = span_v[:, h * HEAD_DIM : (h + 1) * HEAD_DIM]
    dq_block[...] = dq_wide[...].astype(BF16)
    sp_block[...] = sp_head[...].reshape(64, HEAD_DIM).astype(BF16)
    dq_all[t] = dq_block[...]
    sp_all[s // 2, core, c] = sp_block[...]
    sp_pre[0] = sp_head[head]
    local_q.wait()
    for copy in stage:
        copy.wait()

    pl.semaphore_wait(barrier, 26)

    for step in range(1, 16):
        dq_copy(step).start()
    ring_start(0)
    for slot in NEAR[1:]:
        kv_copy(slot).start()
    q_forward(0).start()
    for step in range(1, 4):
        q_copy(step).start()
    for slot in FAR:
        kv_copy(slot).start()
    for slot in range(1, 8):
        sp_copy(slot).start()

    local_cache.wait()
    for step in range(1, 16):
        dq_copy(step).wait_recv()
    row_q = iota((32, 512), 0) % 4
    row_p = iota((32, 512), 1) // 128
    pos = t * 128 + iota((32, 512), 1) % 128
    length = select4(row_p, [len_ref[r] for r in range(4)])
    cache_live = (row_q == row_p) & (pos < length)
    left = iota((32, 128), 1) < 64

    def decode_cached(k, carry):
        column = pl.ds(pl.multiple_of(k * HEAD_DIM, HEAD_DIM), HEAD_DIM)
        queries = dq_all[pl.ds(2 * k, 2)].reshape(32, HEAD_DIM)
        part = jnp.concatenate(
            [dot_nt(queries, cache[r, 0, :, column]) for r in range(4)], axis=1
        )
        part = jnp.where(cache_live, part, NEG)
        top = jnp.max(part, axis=1, keepdims=True)
        part = jnp.exp2((part - top) * EXP2_SCALE)
        total = jnp.sum(part, axis=1, keepdims=True)
        rounded = part.astype(BF16)
        acc = jnp.zeros((32, HEAD_DIM), F32)
        for r in range(4):
            acc += dot_nn(rounded[:, r * 128 : (r + 1) * 128], cache[r, 1, :, column])
        dp_send[pl.ds(2 * k, 2), 0] = acc.reshape(2, 16, HEAD_DIM)
        dp_send[pl.ds(2 * k, 2), 1] = jnp.where(left, top, total).reshape(2, 16, HEAD_DIM)
        return carry

    lax.fori_loop(0, 4, decode_cached, 0, unroll=True)
    for step in (1, 3):
        q_copy(step).wait_recv()
        q_forward(step).start()
    lax.fori_loop(4, 8, decode_cached, 0, unroll=True)
    q_copy(2).wait_recv()
    q_forward(2).start()
    ring_wait(0)
    ring_start(1)

    local_kv.wait()
    offset = off_ref[0]

    def load_queries(slot):
        block = q_all[slot]
        return jnp.concatenate(
            [block[:, h * HEAD_DIM : (h + 1) * HEAD_DIM] for h in range(4)], axis=0
        )

    def attend_block(b, queries, top, side):
        start = (c * 16 + kv_peer(b, -1)) * 256
        part = dot_nt(kv[b, 0], queries)
        part = jnp.where(start + iota((256, 256), 0) < offset, part, NEG)
        scores[side, b] = part
        return jnp.maximum(top, jnp.max(part.reshape(32, 8, 256), axis=0))

    def collect_block(b, top, total, acc, side):
        weights = jnp.exp2((scores[side, b] - top) * EXP2_SCALE)
        total += jnp.sum(weights.reshape(32, 8, 256), axis=0)
        acc += dot_nn(vt[:, b * 256 : (b + 1) * 256], weights.astype(BF16))
        return total, acc

    def transpose_values(slots):
        for slot in slots:
            vt[:, slot * 256 : (slot + 1) * 256] = kv[slot, 1].astype(F32).T.astype(BF16)

    for slot in NEAR[1:]:
        kv_copy(slot).wait_recv()
    transpose_values(NEAR)

    def first_queries(i):
        slot = (2 * i) % 8 + i // 4

        @pl.when(slot % 2 == 1)
        def _():
            q_forward(slot // 2).wait_recv()

        return load_queries(slot)

    def first_step(i, top, side, last=False):
        slot = (2 * i) % 8 + i // 4
        queries = None if last else first_queries(i + 1)
        total, acc = jnp.zeros((8, 256), F32), jnp.zeros((HEAD_DIM, 256), F32)
        later = jnp.full((8, 256), NEG, F32)
        for b in NEAR:
            if not last:
                later = attend_block(b, queries, later, 1 - side)
            total, acc = collect_block(b, top, total, acc, side)
        run_top[slot] = jnp.broadcast_to(top, (8, 256))
        run_total[slot] = total
        run_acc[slot] = acc
        return jnp.max(later, axis=0, keepdims=True)

    def first_steps(i, top):
        return first_step(2 * i + 1, first_step(2 * i, top, 0), 1)

    top = jnp.full((8, 256), NEG, F32)
    queries = load_queries(0)
    for b in NEAR:
        top = attend_block(b, queries, top, 0)
    top = jnp.max(top, axis=0, keepdims=True)
    top = lax.fori_loop(0, 2, first_steps, top)
    ring_wait(1)
    sa_forward().start()
    top = lax.fori_loop(2, 3, first_steps, top)
    top = first_step(6, top, 0)
    first_step(7, top, 1, last=True)

    for slot in range(1, 8):
        sp_copy(slot).wait_recv()
    for slot in FAR:
        kv_copy(slot).wait_recv()
    transpose_values(FAR)
    span_rows = sp_pre[...].reshape(64, HEAD_DIM)
    span_keys = span_rows.astype(BF16)
    span_vt = pltpu.roll(span_rows, 60, axis=0).T.astype(BF16)
    span_row = iota((64, 256), 0)
    span_slot = span_row // 8
    span_y = (y - span_slot // 2 + 4) % 4
    span_x = x + (span_slot % 2) * (3 - 2 * x)
    span_token = (c * 16 + span_y * 4 + span_x) * 4 + span_row % 8
    span_real = span_row % 8 < 4

    def publish(slot, top, total, acc):
        po_send[slot] = acc.astype(BF16)
        row = iota((8, HEAD_DIM), 0)
        tops = jnp.where(row % 2 == 0, top[:, :HEAD_DIM], top[:, HEAD_DIM:])
        totals = jnp.where(row % 2 == 0, total[:, :HEAD_DIM], total[:, HEAD_DIM:])
        ps_send[slot] = jnp.where(row < 2, tops, totals)

    def span_live_at(slot):
        far_c, _ = q_peer(slot, -1)
        return span_real & (span_token <= far_c * 64 + iota((64, 256), 1) % 64)

    def second_slot(i):
        late = jnp.where(i == 7, 4, 6 - i)
        return jnp.where(i < 3, i + 5, jnp.where(i < 5, i - 1, late))

    def second_queries(i, side):
        slot = second_slot(i)
        queries = load_queries(slot)
        part = jnp.where(span_live_at(slot), dot_nt(span_keys, queries), NEG)
        span_scores[side] = part
        top = jnp.maximum(run_top[slot], jnp.max(part.reshape(8, 8, 256), axis=0))
        return queries, top

    def second_step(i, top, side, last=False):
        slot = second_slot(i)
        queries, later = (None, None) if last else second_queries(i + 1, 1 - side)
        factor = jnp.exp2((run_top[slot] - top) * EXP2_SCALE)
        weights = jnp.exp2((span_scores[side] - top) * EXP2_SCALE)
        weights = jnp.where(span_live_at(slot), weights, 0.0)
        total = run_total[slot] * factor + jnp.sum(weights.reshape(8, 8, 256), axis=0)
        acc = run_acc[slot] * factor[0:1] + dot_nn(span_vt, weights.astype(BF16))
        for b in FAR:
            if not last:
                later = attend_block(b, queries, later, 1 - side)
            total, acc = collect_block(b, top, total, acc, side)
        total = jnp.sum(total, axis=0, keepdims=True)
        if last:
            run_top[slot] = jnp.broadcast_to(top, (8, 256))
            run_total[slot] = jnp.broadcast_to(total, (8, 256))
            run_acc[slot] = acc
            return None
        publish(slot, top, total, acc)

        @pl.when(slot != 0)
        def _():
            po_copy(slot).start()
            ps_copy(slot).start()

        return jnp.max(later, axis=0, keepdims=True)

    def second_steps(i, top):
        return second_step(2 * i + 1, second_step(2 * i, top, 0), 1)

    queries, top = second_queries(0, 0)
    for b in FAR:
        top = attend_block(b, queries, top, 0)
    top = jnp.max(top, axis=0, keepdims=True)
    top = lax.fori_loop(0, 3, second_steps, top)
    top = second_step(6, top, 0)
    second_step(7, top, 1, last=True)

    def join(one, other):
        top = jnp.maximum(one[0], other[0])
        left = jnp.exp2((one[0] - top) * EXP2_SCALE)
        right = jnp.exp2((other[0] - top) * EXP2_SCALE)
        return top, one[1] * left + other[1] * right, one[2] * left + other[2] * right

    def unpack(stats):
        top = jnp.concatenate([stats[0:1], stats[1:2]], axis=1)
        return top, jnp.concatenate([stats[2:3], stats[3:4]], axis=1)

    def received(slot):
        po_copy(slot).wait_recv()
        ps_copy(slot).wait_recv()
        return unpack(ps_recv[slot]) + (po_recv[slot].astype(F32),)

    sa_forward().wait_recv()
    sp_wide[...] = sp_all[...].reshape(16, 64, HEAD_DIM).astype(F32)
    new_col = iota((32, 128), 1)
    new_owner = select4(new_col // 32, [own_ref[r] for r in range(4)])
    new_row = (s * 4 + c) * 4 + iota((32, 128), 0) % 4
    new_live = (new_owner == new_row) & (new_col % 8 < 4)

    def decode_fresh(k, carry):
        queries = dq_all[pl.ds(2 * k, 2)].reshape(32, HEAD_DIM)
        fresh = (
            sp_wide[:, pl.ds(pl.multiple_of(8 * k, 8), 8), :].reshape(128, HEAD_DIM).astype(BF16)
        )
        stats = dp_send[pl.ds(2 * k, 2), 1].reshape(32, HEAD_DIM)
        former = stats[:, 0:1]
        part = jnp.where(new_live, dot_nt(queries, fresh), NEG)
        top = jnp.maximum(former, jnp.max(part, axis=1, keepdims=True))
        factor = jnp.exp2((former - top) * EXP2_SCALE)
        part = jnp.where(new_live, jnp.exp2((part - top) * EXP2_SCALE), 0.0)
        total = stats[:, 64:65] * factor + jnp.sum(part, axis=1, keepdims=True)
        acc = dp_send[pl.ds(2 * k, 2), 0].reshape(32, HEAD_DIM) * factor
        acc += dot_nn(pltpu.roll(part, 4, axis=1).astype(BF16), fresh)
        dp_out[pl.ds(2 * k, 2), 0] = acc.astype(BF16).reshape(2, 16, HEAD_DIM)
        pieces = jnp.zeros((32, HEAD_DIM), F32)
        lane = iota((32, HEAD_DIM), 1) // 16
        for first, value in ((0, top), (3, total)):
            for index in range(first, first + 3):
                piece = value.astype(BF16).astype(F32)
                pieces = jnp.where(lane == index, piece, pieces)
                value = value - piece
        dp_out[pl.ds(2 * k, 2), 1] = pieces.astype(BF16).reshape(2, 16, HEAD_DIM)
        return carry

    lax.fori_loop(0, 8, decode_fresh, 0, unroll=True)
    for step in FAR_FIRST:
        dp_copy(step).start()

    publish(4, *join((run_top[4, 0:1, :], run_total[4, 0:1, :], run_acc[4]), received(5)))
    po_copy(4).start()
    ps_copy(4).start()

    state = unpack(ps_send[0]) + (po_send[0].astype(F32),)
    for slot in (1, 6, 7, 2, 3):
        state = join(state, received(slot))

    _, total, acc = join(state, received(4))
    result = (acc / total).T
    for h in range(4):
        out_ref[0, :, h * HEAD_DIM : (h + 1) * HEAD_DIM] = result[h * 64 : (h + 1) * 64].astype(BF16)

    for step in range(1, 16):
        dp_copy(step).wait_recv()
    dp_recv[0] = dp_out[t]
    stats = [dp_recv[i, 1].astype(F32) for i in range(16)]
    tops = [v[:, 0:1] + v[:, 16:17] + v[:, 32:33] for v in stats]
    totals = [v[:, 48:49] + v[:, 64:65] + v[:, 80:81] for v in stats]
    top = tops[0]
    for i in range(1, 16):
        top = jnp.maximum(top, tops[i])
    acc = jnp.zeros((16, HEAD_DIM), F32)
    total = jnp.zeros((16, 1), F32)
    for i in range(16):
        factor = jnp.exp2((tops[i] - top) * EXP2_SCALE)
        acc += dp_recv[i, 0].astype(F32) * factor
        total += totals[i] * factor
    d_result[...] = acc / total
    for h in range(4):
        dout_ref[:, h * HEAD_DIM : (h + 1) * HEAD_DIM] = d_result[4 * h : 4 * h + 4, :].astype(BF16)

    for step in range(1, 16):
        dq_copy(step).wait_send()
        dp_copy(step).wait_send()
    for step in range(4):
        q_forward(step).wait_send()
    for step in range(1, 4):
        q_copy(step).wait_send()
    for step in range(2):
        for copy in ring_copies(step):
            copy.wait_send()
    sa_forward().wait_send()
    for slot in range(1, 8):
        kv_copy(slot).wait_send()
        sp_copy(slot).wait_send()
        po_copy(slot).wait_send()
        ps_copy(slot).wait_send()


def body(
    span_queries,
    prompt_cache,
    span_kv,
    span_offsets,
    decode_queries,
    decode_cache,
    cache_lengths,
    owner_rows,
):
    vmem = pl.BlockSpec(memory_space=pltpu.VMEM)
    hbm = pl.BlockSpec(memory_space=pltpu.HBM)
    sem = pltpu.SemaphoreType.DMA
    return pl.pallas_call(
        kernel,
        out_shape=(
            pltpu.VMEM(span_queries.shape, BF16),
            pltpu.VMEM(decode_queries.shape, BF16),
        ),
        in_specs=[hbm] * 8,
        out_specs=(vmem, vmem),
        scratch_shapes=[
            pltpu.SMEM((1,), jnp.int32),
            pltpu.SMEM((4,), jnp.int32),
            pltpu.SMEM((4,), jnp.int32),
            pltpu.VMEM((4, 512), BF16),
            pltpu.VMEM((1, 2, 4, 1024), BF16),
            pltpu.VMEM((4, 2, 128, 1024), BF16),
            pltpu.VMEM((8, 2, 256, HEAD_DIM), BF16),
            pltpu.VMEM((8, 2, 256, HEAD_DIM), BF16),
            pltpu.VMEM((HEAD_DIM, 2048), BF16),
            pltpu.VMEM((8, 64, 512), BF16),
            pltpu.VMEM((2, 8, 256, 256), F32),
            pltpu.VMEM((2, 64, 256), F32),
            pltpu.VMEM((8, 8, 256), F32),
            pltpu.VMEM((8, 8, 256), F32),
            pltpu.VMEM((8, HEAD_DIM, 256), F32),
            pltpu.VMEM((8, HEAD_DIM, 256), BF16),
            pltpu.VMEM((8, HEAD_DIM, 256), BF16),
            pltpu.VMEM((8, 8, HEAD_DIM), F32),
            pltpu.VMEM((8, 8, HEAD_DIM), F32),
            pltpu.VMEM((8, 8, HEAD_DIM), F32),
            pltpu.VMEM((8, 8, HEAD_DIM), F32),
            pltpu.VMEM((64, HEAD_DIM), BF16),
            pltpu.VMEM((2, 2, 4, 64, HEAD_DIM), BF16),
            pltpu.VMEM((16, 64, HEAD_DIM), F32),
            pltpu.VMEM((16, HEAD_DIM), F32),
            pltpu.VMEM((16, HEAD_DIM), BF16),
            pltpu.VMEM((16, 16, HEAD_DIM), BF16),
            pltpu.VMEM((16, 2, 16, HEAD_DIM), F32),
            pltpu.VMEM((16, 2, 16, HEAD_DIM), BF16),
            pltpu.VMEM((16, 2, 16, HEAD_DIM), BF16),
            pltpu.VMEM((16, HEAD_DIM), F32),
            sem((8,)),
            sem((8,)),
            sem((8,)),
            sem((8,)),
            sem((8,)),
            sem((8,)),
            sem((8,)),
            sem((8,)),
            sem(()),
            sem(()),
            sem((8,)),
            sem((8,)),
            sem((16,)),
            sem((16,)),
            sem((16,)),
            sem((16,)),
            sem((8,)),
            sem((8,)),
            sem((8,)),
            sem((8,)),
        ],
        compiler_params=pltpu.CompilerParams(
            collective_id=0, has_side_effects=True, vmem_limit_bytes=60 * 1024 * 1024
        ),
    )(
        span_offsets,
        cache_lengths,
        owner_rows,
        decode_queries,
        span_kv,
        span_queries,
        prompt_cache,
        decode_cache,
    )


def solution(mesh):
    return jax.shard_map(
        body,
        mesh=mesh,
        in_specs=(
            P("sect", "ctx", "tp"),
            P("sect", None, ("ctx", "tp"), None),
            P("sect", None, ("ctx", "tp"), None),
            P("sect"),
            P(("sect", "ctx"), "tp"),
            P(("sect", "ctx"), None, "tp", None),
            P(("sect", "ctx")),
            P(),
        ),
        out_specs=(P("sect", "ctx", "tp"), P(("sect", "ctx"), "tp")),
        check_vma=False,
    )
```
